128 devices in a mesh: seq: 32 (over x, y, core), blk: 4 (over z).
Axes of the slice: x: 4, y: 4, z: 4, core: 2. Of those that a mesh axis runs over, the one named last changes fastest.
Arguments:
- nodes: bfloat16 [16384, 1024], P(('seq', 'blk')), may hold values from -21 to 21
- w_qkv: bfloat16 [1024, 3072], replicated, may hold values from -0.1875 to 0.1875
- w_out: bfloat16 [1024, 1024], replicated, may hold values from -0.1875 to 0.1875
- perm: int32 [16384], P('seq'), may hold values from 0 to 16383, as said below
- blocks: int32 [128, 8], P('seq'), may hold values from 0 to 127, as said below
- grad_out: bfloat16 [16384, 1024], P(('seq', 'blk')), may hold values from -24 to 24
Outputs:
- out: bfloat16 [16384, 1024], P(('seq', 'blk'))
- grad_nodes: bfloat16 [16384, 1024], P(('seq', 'blk'))
- w_out_grad: float32 [1024, 1024], P(('seq', 'blk'))
The draws below stay inside these ranges and needn't reach their ends.
Inputs may be any that keep to these rules, and one draw needn't show every extreme that they name: perm is a permutation that maps each aligned run of 512 positions onto itself. Within each aligned run of 4 rows (query blocks), at most 2 entries name blocks of any one aligned run of 4 key blocks; the run with the same index is named exactly 2 times, and one run, the same for all, is named exactly 2 times by every run of rows.
All inputs are finite; a program needn't handle non-finite values.
Results may differ from the reference program's by a relative error of at most 0.023.
The reference program's roundings to bfloat16 on the way count: a program that leaves them out, or rounds other values in their place, can miss the bound.
Values may be sent and summed in bfloat16 or wider, within the bound.
A program may use at most 128 MiB of HBM per device.

```python
import jax
import jax.numpy as jnp
from jax import lax

D = 1024
HEADS = 16
HDIM = 64
QB = 128
KSLOTS = 8
GROUP = 512
QBG = 4
NODES = 16384
BLOCKS = 128
CAP = 2


def draw_nodes(key, part):
    key = jax.random.fold_in(key, 11)
    raw_values = jax.random.normal(key, (NODES, D), jnp.float32)
    return jnp.clip(raw_values, -6.0, 6.0).astype(jnp.bfloat16)


def draw_perm(key, part):
    key = jax.random.fold_in(key, 5)
    windows = NODES // GROUP

    def draw_window(window):
        shuffled = jax.random.permutation(jax.random.fold_in(key, window), GROUP).astype(jnp.int32)
        return window * GROUP + shuffled
    return jax.vmap(draw_window)(jnp.arange(windows, dtype=jnp.int32)).reshape(NODES).astype(jnp.int32)


def draw_blocks(key, part):
    key = jax.random.fold_in(key, 7)
    groups = NODES // GROUP
    entries = QBG * KSLOTS
    pool_size = groups * CAP
    hub_group = jax.random.randint(jax.random.fold_in(key, 1), (), 0, groups)

    def draw_group(group_id):
        group_key = jax.random.fold_in(key, group_id + 2)
        key_rank, key_mix, key_local = jax.random.split(group_key, 3)
        pool_index = jnp.arange(pool_size, dtype=jnp.int32)
        pool_owner = pool_index // CAP
        forced = (pool_owner == group_id) | (pool_owner == hub_group)
        ranked = jax.random.randint(key_rank, (pool_size,), 0, 1 << 20) * pool_size + pool_index
        ranked = ranked + jnp.where(forced, 1 << 30, 0)
        chosen = lax.top_k(ranked, entries)[1]
        owners = jax.random.permutation(key_mix, chosen // CAP)
        local_ids = jax.random.randint(key_local, (entries,), 0, QBG)
        return (owners * QBG + local_ids).reshape(QBG, KSLOTS)
    listed = jax.vmap(draw_group)(jnp.arange(groups, dtype=jnp.int32))
    return listed.reshape(groups * QBG, KSLOTS).astype(jnp.int32)


def with_spikes(array, stream_key, source, target, blocks, factor):
    owner, partner = [(jnp.arange(array.shape[axis_at]) // (array.shape[axis_at] // blocks)).reshape([-1 if axis == axis_at else 1 for axis in range(array.ndim)]) for axis_at in (source, target)]
    chosen = jax.random.permutation(stream_key, blocks)[partner]
    strong = (owner == chosen) | (owner == (partner + blocks // 2) % blocks)
    return jnp.where(strong, factor * array, array)


def block_scale(stream_key, shape, shards, smallest, high):
    factor_of = 1.0
    for dim, parts in shards:
        draws = jax.random.uniform(jax.random.fold_in(jax.random.fold_in(stream_key, 6), dim), (parts,), jnp.float32, smallest / len(shards), high / len(shards))
        factor_of = factor_of * jnp.repeat(jnp.exp(draws), shape[dim] // parts).reshape((-1,) + (1,) * (len(shape) - 1 - dim))
    return factor_of


def centred(stream_key, extent, width, most, cuts=(), kind=jnp.bfloat16):
    values = jax.random.normal(stream_key, extent, jnp.float32) * width
    if len(cuts) > 0:
        values = block_scale(stream_key, extent, cuts, -0.22, 0.18) * values
    return jnp.clip(values, min=-most, max=most).astype(kind)


def heavy_noise(rng, dims, spread, most, cuts, heavy, kind=jnp.bfloat16):
    values = spread * jax.random.normal(rng, dims, jnp.float32)
    if cuts:
        values = values * block_scale(rng, dims, cuts, -0.22, 0.18)
    return jnp.clip(with_spikes(values, jax.random.fold_in(rng, 3), *heavy), -most, most).astype(kind)


def setup_inputs(seed: int = 0) -> dict:
    keys = jax.random.split(jax.random.key(seed), 7)
    nodes = draw_nodes(jax.random.fold_in(keys[6], 71), 0)
    w_qkv = centred(keys[1], (D, 3 * D), D ** -0.5, 0.1875)
    w_out = centred(keys[2], (D, D), D ** -0.5, 0.1875)
    perm = draw_perm(jax.random.fold_in(keys[6], 71), 0)
    blocks = draw_blocks(jax.random.fold_in(keys[6], 71), 0)
    grad_out = heavy_noise(keys[5], (NODES, D), 1.0, 24.0, ((0, 128),), (0, 1, 128, 5.5))
    return dict(nodes=nodes, w_qkv=w_qkv, w_out=w_out, perm=perm, blocks=blocks, grad_out=grad_out)


def softmax_rows(scores):
    row_top = jnp.max(scores, axis=-1, keepdims=True)
    raised = jnp.exp(scores - row_top)
    return raised / jnp.sum(raised, axis=-1, keepdims=True)


def rounded(values):
    return lax.optimization_barrier(values.astype(jnp.bfloat16))


def reference(nodes, w_qkv, w_out, perm, blocks, grad_out):
    score_scale = HDIM ** -0.5
    projected = jnp.dot(nodes, w_qkv, preferred_element_type=jnp.float32).astype(jnp.bfloat16)
    ordered = projected[perm]
    query_c = ordered[:, :D].reshape(BLOCKS, QB, HEADS, HDIM)
    key_c = ordered[:, D:2 * D].reshape(BLOCKS, QB, HEADS, HDIM)
    value_c = ordered[:, 2 * D:].reshape(BLOCKS, QB, HEADS, HDIM)

    def attend(query_blk, listed):
        key_rows = key_c[listed].reshape(KSLOTS * QB, HEADS, HDIM).astype(jnp.float32)
        value_rows = value_c[listed].reshape(KSLOTS * QB, HEADS, HDIM).astype(jnp.float32)
        scores = jnp.einsum("qhd,khd->hqk", query_blk.astype(jnp.float32), key_rows) * score_scale
        probs = softmax_rows(scores)
        probs_low = rounded(probs).astype(jnp.float32)
        attended = jnp.einsum("hqk,khd->qhd", probs_low, value_rows).astype(jnp.bfloat16)
        return key_rows, value_rows, probs, probs_low, attended

    def forward_block(block_item):
        return attend(block_item[0], block_item[1])[4]

    attended_c = lax.map(forward_block, (query_c, blocks))
    mixed = jnp.zeros((NODES, D), jnp.bfloat16).at[perm].set(attended_c.reshape(NODES, D))
    out = jnp.dot(mixed, w_out, preferred_element_type=jnp.float32).astype(jnp.bfloat16)

    grad_mixed = jnp.dot(grad_out, w_out.T, preferred_element_type=jnp.float32).astype(jnp.bfloat16)
    w_out_grad = jnp.dot(grad_out.T, mixed, preferred_element_type=jnp.float32)
    grad_c = grad_mixed[perm].reshape(BLOCKS, QB, HEADS, HDIM)

    def backward_block(running, block_item):
        key_acc, value_acc = running
        query_blk, listed, grad_blk, attended_blk = block_item
        key_rows, value_rows, probs, probs_low, unused_out = attend(query_blk, listed)
        grad_f = grad_blk.astype(jnp.float32)
        grad_scores = jnp.einsum("qhd,khd->hqk", grad_f, value_rows)
        row_delta = jnp.sum(grad_f * attended_blk.astype(jnp.float32), axis=-1).T[:, :, None]
        grad_logits = rounded(probs * (grad_scores - row_delta)).astype(jnp.float32)
        grad_query = (jnp.einsum("hqk,khd->qhd", grad_logits, key_rows) * score_scale).astype(jnp.bfloat16)
        key_part = (jnp.einsum("hqk,qhd->khd", grad_logits, query_blk.astype(jnp.float32)) * score_scale).astype(jnp.bfloat16)
        value_part = jnp.einsum("hqk,qhd->khd", probs_low, grad_f).astype(jnp.bfloat16)
        key_acc = key_acc.at[listed].add(key_part.astype(jnp.float32).reshape(KSLOTS, QB, HEADS, HDIM))
        value_acc = value_acc.at[listed].add(value_part.astype(jnp.float32).reshape(KSLOTS, QB, HEADS, HDIM))
        return (key_acc, value_acc), grad_query

    zero_acc = jnp.zeros((BLOCKS, QB, HEADS, HDIM), jnp.float32)
    sums, grad_query_c = lax.scan(backward_block, (zero_acc, zero_acc), (query_c, blocks, grad_c, attended_c))
    grad_key_c = sums[0].astype(jnp.bfloat16).reshape(NODES, D)
    grad_value_c = sums[1].astype(jnp.bfloat16).reshape(NODES, D)
    grad_ordered = jnp.concatenate([grad_query_c.reshape(NODES, D), grad_key_c, grad_value_c], axis=1)
    grad_projected = jnp.zeros((NODES, 3 * D), jnp.bfloat16).at[perm].set(grad_ordered)
    grad_nodes = jnp.dot(grad_projected, w_qkv.T, preferred_element_type=jnp.float32).astype(jnp.bfloat16)
    return out, grad_nodes, w_out_grad
```

```python
import jax
import jax.numpy as jnp
from jax import lax
from jax.experimental import pallas as pl
from jax.experimental.pallas import tpu as pltpu
from jax.sharding import PartitionSpec as P

HDIM = 64
QB = 128
GROUP = 512
SIDE = 4
BF = jnp.bfloat16
F32 = jnp.float32
MESH = pl.DeviceIdType.MESH
VMEM_BYTES = 56 * 1024 * 1024


def place():
    s = lax.axis_index("seq")
    z = lax.axis_index("blk")
    return s // 8, (s // 2) % 4, s % 2, z


def seq_of(x, y, c):
    return x * 8 + y * 2 + c


def turn(i, d):
    return lax.rem(i + (d + SIDE), SIDE)


def greet(x, y, c, z, y_steps):
    barrier = pltpu.get_barrier_semaphore()
    others = [(seq_of(x, y, c), turn(z, d)) for d in (1, 2, 3)]
    others += [(seq_of(turn(x, d), y, c), z) for d in (1, 2, 3)]
    others += [(seq_of(x, turn(y, d), c), z) for d in y_steps]
    others += [(seq_of(x, y, 1 - c), z)]
    for other in others:
        pl.semaphore_signal(barrier, inc=1, device_id=other, device_id_type=MESH)
    return lambda: pl.semaphore_wait(barrier, len(others))


def remote(src, dst, send_sem, recv_sem, device):
    return pltpu.make_async_remote_copy(
        src_ref=src,
        dst_ref=dst,
        send_sem=send_sem,
        recv_sem=recv_sem,
        device_id=device,
        device_id_type=MESH,
    )


def interleave(a, b):
    low = lax.broadcasted_iota(jnp.int32, a.shape, 1) < HDIM
    return (
        jnp.where(low, a, pltpu.roll(b, HDIM, 1)),
        jnp.where(low, pltpu.roll(a, HDIM, 1), b),
    )


def dot(a, b, ca=1, cb=0):
    return lax.dot_general(a, b, (((ca,), (cb,)), ((), ())), preferred_element_type=F32)


def store_pairs(ref, a, b):
    for half in range(2):
        cols = slice(128 * half, 128 * half + 128)
        first, second = interleave(a[:, cols], b[:, cols])
        ref[:, 256 * half : 256 * half + 128] = first.astype(BF)
        ref[:, 256 * half + 128 : 256 * half + 256] = second.astype(BF)


def gather_kernel(
    nodes, w_qkv, w_out, go, perm, blk, kv_all, qg_all, blk_all,
    wbuf, wobuf, pick, zs_kv, zr_kv, zs_qg, zr_qg, xs_kv, xs_qg,
    w_sem, zs_sem, zr_sem, xs_sem, xr_sem, ys_sem, yr_sem, cs_sem, cr_sem,
):
    x, y, c, z = place()
    group = seq_of(x, y, c)
    kv_cols = pl.ds(1024, 2048)
    load_kv = pltpu.make_async_copy(w_qkv.at[:, kv_cols], wbuf.at[:, kv_cols], w_sem.at[0])
    load_q = pltpu.make_async_copy(w_qkv.at[:, pl.ds(0, 1024)], wbuf.at[:, pl.ds(0, 1024)], w_sem.at[1])
    load_o = pltpu.make_async_copy(w_out, wobuf, w_sem.at[2])
    load_kv.start()
    load_q.start()
    load_o.start()
    ready = greet(x, y, c, z, (1, 3))

    local = perm[...] - group * GROUP
    hits = lax.broadcasted_iota(jnp.int32, (GROUP, GROUP), 0) == local
    pick[...] = jnp.where(hits, 1.0, 0.0).T.astype(BF)

    def z_copy(which, d):
        src, dst = ((zs_kv, zr_kv), (zs_qg, zr_qg))[which]
        to = turn(z, d)
        return remote(
            src.at[to], dst.at[pl.ds(pl.multiple_of(z * QB, QB), QB)],
            zs_sem.at[which, d - 1], zr_sem.at[which, d - 1], (group, to),
        )

    own_rows = pl.ds(pl.multiple_of(z * QB, QB), QB)
    load_kv.wait()
    for d in (2, 1, 3, 0):
        to = turn(z, d)
        off = pl.multiple_of(to * 256, 256)
        k = dot(nodes[...], wbuf[:, pl.ds(1024 + off, 256)])
        v = dot(nodes[...], wbuf[:, pl.ds(2048 + off, 256)])
        if d == 2:
            ready()
        if d:
            store_pairs(zs_kv.at[to], k, v)
            z_copy(0, d).start()
        else:
            store_pairs(zr_kv.at[own_rows], k, v)

    blk_copies = [
        remote(blk, blk_all.at[x], xs_sem.at[2, d - 1], xr_sem.at[2, d - 1], (seq_of(turn(x, d), y, c), z))
        for d in (1, 2, 3)
    ]
    for copy in blk_copies:
        copy.start()
    blk_all[x] = blk[...]

    load_q.wait()
    load_o.wait()
    for d in (2, 1, 3, 0):
        to = turn(z, d)
        off = pl.multiple_of(to * 256, 256)
        q = dot(nodes[...], wbuf[:, pl.ds(off, 256)])
        g = dot(go[...], wobuf[pl.ds(off, 256), :], 1, 1)
        if d:
            store_pairs(zs_qg.at[to], q, g)
            z_copy(1, d).start()
        else:
            store_pairs(zr_qg.at[own_rows], q, g)

    def to_cluster(rows, staged):
        ordered = dot(pick[...], rows[...])
        for h in range(SIDE):
            staged[h] = ordered[:, 128 * h : 128 * h + 128].astype(BF)

    def x_copy(which, d):
        to = turn(x, d)
        src = (xs_kv, xs_qg)[which].at[to]
        dst = kv_all.at[group] if which == 0 else qg_all.at[x]
        return remote(src, dst, xs_sem.at[which, d - 1], xr_sem.at[which, d - 1], (seq_of(to, y, c), z))

    def y_copy(d, k):
        mine = kv_all.at[seq_of(turn(x, -d), y, c)]
        to = seq_of(x, turn(y, (1, 3)[k]), c)
        return remote(mine, mine, ys_sem.at[d, k], yr_sem.at[d, k], (to, z))

    def pass_on(d):
        y_copy(d, 0).start()
        y_copy(d, 1).start()
        cross(d, 0).start()

    def relay(d, k):
        rows = pl.ds(256 * k, 256)
        step = (1, 3)[k]
        got = kv_all.at[seq_of(turn(x, -d), turn(y, -step), c), rows]
        return remote(got, got, ys_sem.at[d, 2 + k], yr_sem.at[d, 2 + k], (seq_of(x, turn(y, step), c), z))

    def cross(d, k):
        got = kv_all.at[seq_of(turn(x, -d), turn(y, -k), c)]
        return remote(got, got, cs_sem.at[d, k], cr_sem.at[d, k], (seq_of(x, y, 1 - c), z))

    for d in (1, 2, 3):
        z_copy(0, d).wait_recv()
    to_cluster(zr_kv, xs_kv)
    for d in (2, 1, 3):
        x_copy(0, d).start()
    kv_all[group] = xs_kv[x]
    pass_on(0)

    for d in (1, 3):
        x_copy(0, d).wait_recv()
        pass_on(d)

    for d in (1, 2, 3):
        z_copy(1, d).wait_recv()
    to_cluster(zr_qg, xs_qg)
    for d in (2, 1, 3):
        x_copy(1, d).start()
    qg_all[x] = xs_qg[x]

    x_copy(0, 2).wait_recv()
    pass_on(2)

    for d in (0, 1, 3, 2):
        for k in range(2):
            y_copy(d, k).wait_recv()
            relay(d, k).start()
            cross(d, (1, 3)[k]).start()
    for d in (0, 1, 3, 2):
        relay(d, 0).wait_recv()
        relay(d, 1).wait_recv()
        cross(d, 2).start()

    for d in (1, 2, 3):
        x_copy(1, d).wait_recv()
        blk_copies[d - 1].wait_recv()
    for d in range(SIDE):
        for k in range(SIDE):
            cross(d, k).wait_recv()
    for d in (1, 2, 3):
        for which in range(2):
            z_copy(which, d).wait_send()
            x_copy(which, d).wait_send()
        blk_copies[d - 1].wait_send()
    for d in range(SIDE):
        for k in range(2):
            y_copy(d, k).wait_send()
            relay(d, k).wait_send()
        for k in range(SIDE):
            cross(d, k).wait_send()


def attention_kernel(listed, kv_all, qg_all, dkv_all, dqa_all, keys, acc):
    acc[...] = jnp.zeros_like(acc)
    low = lax.broadcasted_iota(jnp.int32, (QB, QB), 1) < HDIM
    top = lax.broadcasted_iota(jnp.int32, (QB, QB), 0) < HDIM

    def step(j, carry):
        ids = [listed[j // 4, j % 4, t] for t in range(8)]
        for t in range(8):
            keys[t * QB : (t + 1) * QB] = kv_all[ids[t]]
        qg = qg_all[j].astype(F32)
        both = jnp.concatenate(
            [jnp.where(low, qg * HDIM ** (-0.5), 0.0), jnp.where(low, 0.0, qg)], axis=0
        ).astype(BF)
        rows = dot(keys[...], both, 1, 1)
        scores, grad_scores = rows[:, :QB], rows[:, QB:]
        raised = jnp.exp(scores - jnp.max(scores, axis=0, keepdims=True))
        probs = raised / jnp.sum(raised, axis=0, keepdims=True)
        probs_low = probs.astype(BF)
        attended = dot(keys[...], probs_low, 0, 0)
        kept = attended.astype(BF).astype(F32)
        delta = jnp.sum(jnp.where(top, 0.0, qg.T * kept), axis=0, keepdims=True)
        grad_logits = (probs * (grad_scores - delta)).astype(BF)
        grad_query = dot(keys[...], grad_logits, 0, 0) * HDIM ** (-0.5)
        dqa_all[j] = jnp.where(top, grad_query, attended).T.astype(BF)
        parts = dot(jnp.concatenate([grad_logits, probs_low], axis=1), both)
        for t in range(8):
            acc[ids[t]] += parts[t * QB : (t + 1) * QB]
        return carry

    lax.fori_loop(0, 16, step, 0)

    def finish(b, carry):
        dkv_all[b] = acc[b].astype(BF)
        return carry

    lax.fori_loop(0, 128, finish, 0)


def scatter_kernel(
    dkv, dqa, w_qkv, w_out, go, perm, out, grad_nodes, w_grad,
    wbuf, wobuf, place_hits, side, opp, y_recv, y_send, xs_kv, xr_kv, xr_qa, zs_kv, zr_kv, zs_qa, zr_qa,
    mixed, gproj, wpart, wc_send, wc_recv, wz_send, wz_recv, wx_send, wx_recv, wy_send, wy_recv,
    w_sem, zs_sem, zr_sem, xs_sem, xr_sem, ys_sem, yr_sem, cs_sem, cr_sem, ws_sem, wr_sem,
):
    x, y, c, z = place()
    group = seq_of(x, y, c)
    load_o = pltpu.make_async_copy(w_out, wobuf, w_sem.at[0])
    load_w = pltpu.make_async_copy(w_qkv, wbuf, w_sem.at[1])
    load_o.start()
    load_w.start()
    ready = greet(x, y, c, z, (1, 2, 3))
    sibling = (seq_of(x, y, 1 - c), z)

    def cross(d, k):
        xt, yt = turn(x, d), turn(y, k)
        return remote(dkv.at[seq_of(xt, yt, 1 - c)], side.at[d, k], cs_sem.at[d, k], cr_sem.at[d, k], sibling)

    def x_copy(which, d):
        to = turn(x, d)
        src = xs_kv.at[to] if which == 0 else dqa.at[to]
        dst = (xr_kv, xr_qa)[which].at[:, pl.ds(pl.multiple_of(x * 128, 128), 128)]
        return remote(src, dst, xs_sem.at[which, d - 1], xr_sem.at[which, d - 1], (seq_of(to, y, c), z))

    def z_copy(which, d):
        to = turn(z, d)
        src, dst = ((zs_kv, zr_kv), (zs_qa, zr_qa))[which]
        return remote(
            src.at[pl.ds(pl.multiple_of(to * QB, QB), QB)], dst.at[z],
            zs_sem.at[which, d - 1], zr_sem.at[which, d - 1], (group, to),
        )

    def opposite(d, k):
        step = (1, 3)[k]
        rows = pl.ds(256 * k, 256)
        return remote(
            opp.at[d, rows], opp.at[SIDE + d, rows], ys_sem.at[d, k], yr_sem.at[d, k],
            (seq_of(x, turn(y, step), c), z),
        )

    def beside(d, k):
        step = (1, 3)[k]
        return remote(
            y_send.at[d, k], y_recv.at[d, k], ys_sem.at[d, 2 + k], yr_sem.at[d, 2 + k],
            (seq_of(x, turn(y, step), c), z),
        )

    def paired(d, k):
        cross(d, k).wait_recv()
        return dkv[seq_of(turn(x, d), turn(y, k), c)].astype(F32) + side[d, k].astype(F32)

    order = (2, 1, 3, 0)
    ready()
    for k in (2, 1, 3, 0):
        for d in order:
            cross(d, k).start()
    for d in (2, 1, 3):
        x_copy(1, d).start()
    local = perm[...] - group * GROUP
    hits = lax.broadcasted_iota(jnp.int32, (GROUP, GROUP), 0) == local
    place_hits[...] = jnp.where(hits, 1.0, 0.0).astype(BF)
    own_cols = pl.ds(pl.multiple_of(x * 128, 128), 128)
    own_rows = pl.ds(pl.multiple_of(z * QB, QB), QB)

    for d in order:
        opp[d] = paired(d, 2).astype(BF)
        opposite(d, 0).start()
        opposite(d, 1).start()

    xr_qa[:, own_cols] = dqa[x]
    for d in (1, 2, 3):
        x_copy(1, d).wait_recv()
    zs_qa[...] = dot(place_hits[...], xr_qa[...]).astype(BF)
    for d in (2, 1, 3):
        z_copy(1, d).start()
    zr_qa[z] = zs_qa[own_rows]

    for d in order:
        for k in range(2):
            total = paired(d, (1, 3)[k])
            opposite(d, k).wait_recv()
            rows = slice(256 * k, 256 * k + 256)
            rest = slice(256 - 256 * k, 512 - 256 * k)
            y_send[d, k, rows] = (total[rows] + opp[SIDE + d, rows].astype(F32)).astype(BF)
            y_send[d, k, rest] = total[rest].astype(BF)
            beside(d, k).start()

    for d in (1, 2, 3):
        z_copy(1, d).wait_recv()
    for h in range(SIDE):
        for half in range(2):
            a = zr_qa[h, :, 256 * half : 256 * half + 128].astype(F32)
            b = zr_qa[h, :, 256 * half + 128 : 256 * half + 256].astype(F32)
            cols = slice(256 * h + 128 * half, 256 * h + 128 * half + 128)
            first, second = interleave(a, b)
            gproj[:, cols] = first.astype(BF)
            mixed[:, cols] = second.astype(BF)
    load_o.wait()
    out[...] = dot(mixed[...], wobuf[...]).astype(BF)
    for i in range(SIDE):
        part = dot(go[:, 256 * i : 256 * i + 256], mixed[...], 0, 0)
        wpart[4 * i : 4 * i + 4] = part.reshape(4, 2, 32, 1024)

    def w_rows(core, to):
        return wpart[:, core, pl.ds(pl.multiple_of(to * 8, 8), 8), :].reshape(QB, 1024)

    w_cross = remote(wc_send, wc_recv, ws_sem.at[0], wr_sem.at[0], sibling)
    for to in range(SIDE):
        wc_send[to] = w_rows(1 - c, to).astype(BF)
    w_cross.start()

    for d in order:
        for k in range(2):
            beside(d, k).wait_recv()
        total = paired(d, 0) + (y_recv[d, 0].astype(F32) + y_recv[d, 1].astype(F32))
        if d:
            xs_kv[turn(x, d)] = total.astype(BF)
            x_copy(0, d).start()
        else:
            xr_kv[:, own_cols] = total.astype(BF)

    def w_z(d):
        return remote(
            wz_send.at[d - 1], wz_recv.at[d - 1], ws_sem.at[d], wr_sem.at[d], (group, turn(z, d))
        )

    def w_x(d):
        return remote(
            wx_send.at[pl.ds(pl.multiple_of(turn(x, d) * 32, 32), 32)], wx_recv.at[d - 1],
            ws_sem.at[3 + d], wr_sem.at[3 + d], (seq_of(turn(x, d), y, c), z),
        )

    def w_y(d):
        return remote(
            wy_send.at[turn(y, d)], wy_recv.at[d - 1],
            ws_sem.at[6 + d], wr_sem.at[6 + d], (seq_of(x, turn(y, d), c), z),
        )

    w_cross.wait_recv()
    for d in (2, 1, 3):
        to = turn(z, d)
        wz_send[d - 1] = (w_rows(c, to) + wc_recv[to].astype(F32)).astype(BF)
        w_z(d).start()

    for d in (1, 2, 3):
        x_copy(0, d).wait_recv()
    zs_kv[...] = dot(place_hits[...], xr_kv[...]).astype(BF)
    for d in (2, 1, 3):
        z_copy(0, d).start()
    zr_kv[z] = zs_kv[own_rows]

    wsum = w_rows(c, z) + wc_recv[z].astype(F32)
    for d in (1, 2, 3):
        w_z(d).wait_recv()
        wsum += wz_recv[d - 1].astype(F32)
    wx_send[...] = wsum.astype(BF)
    for d in (2, 1, 3):
        w_x(d).start()

    for d in (1, 2, 3):
        z_copy(0, d).wait_recv()
    for h in range(SIDE):
        for half in range(2):
            a = zr_kv[h, :, 256 * half : 256 * half + 128].astype(F32)
            b = zr_kv[h, :, 256 * half + 128 : 256 * half + 256].astype(F32)
            col = 256 * h + 128 * half
            first, second = interleave(a, b)
            gproj[:, 1024 + col : 1024 + col + 128] = first.astype(BF)
            gproj[:, 2048 + col : 2048 + col + 128] = second.astype(BF)
    load_w.wait()
    for i in range(SIDE):
        rows = slice(256 * i, 256 * i + 256)
        grad_nodes[:, rows] = dot(gproj[...], wbuf[rows, :], 1, 1).astype(BF)

    wrows = wx_send[pl.ds(pl.multiple_of(x * 32, 32), 32)].astype(F32)
    for d in (1, 2, 3):
        w_x(d).wait_recv()
        wrows += wx_recv[d - 1].astype(F32)
    wy_send[...] = wrows.reshape(SIDE, 8, 1024)
    for d in (2, 1, 3):
        w_y(d).start()
    wfinal = wy_send[y]
    for d in (1, 2, 3):
        w_y(d).wait_recv()
        wfinal += wy_recv[d - 1]
    w_grad[...] = wfinal

    w_cross.wait_send()
    for d in (1, 2, 3):
        for which in range(2):
            x_copy(which, d).wait_send()
            z_copy(which, d).wait_send()
        w_z(d).wait_send()
        w_x(d).wait_send()
        w_y(d).wait_send()
    for d in range(SIDE):
        for k in range(SIDE):
            cross(d, k).wait_send()
        for k in range(2):
            opposite(d, k).wait_send()
            beside(d, k).wait_send()


def dma(*shape):
    return pltpu.SemaphoreType.DMA(shape)


def on_device(nodes, w_qkv, w_out, perm, blocks, grad_out):
    vm = pl.BlockSpec(memory_space=pltpu.VMEM)
    anywhere = pl.BlockSpec(memory_space=pl.ANY)
    sds = jax.ShapeDtypeStruct
    perm_row = perm.reshape(1, GROUP)
    blk = jnp.pad(blocks, ((0, 4), (0, 120)))
    kv_all, qg_all, blk_all = pl.pallas_call(
        gather_kernel,
        out_shape=(sds((32, GROUP, 128), BF), sds((SIDE, GROUP, 128), BF), sds((SIDE, 8, 128), jnp.int32)),
        in_specs=[vm, anywhere, anywhere, vm, vm, vm],
        out_specs=(vm, vm, vm),
        scratch_shapes=[
            pltpu.VMEM((1024, 3072), BF),
            pltpu.VMEM((1024, 1024), BF),
            pltpu.VMEM((GROUP, GROUP), BF),
            pltpu.VMEM((SIDE, QB, 512), BF),
            pltpu.VMEM((GROUP, 512), BF),
            pltpu.VMEM((SIDE, QB, 512), BF),
            pltpu.VMEM((GROUP, 512), BF),
            pltpu.VMEM((SIDE, GROUP, 128), BF),
            pltpu.VMEM((SIDE, GROUP, 128), BF),
            dma(3), dma(2, 3), dma(2, 3), dma(3, 3), dma(3, 3),
            dma(4, 4), dma(4, 4), dma(4, 4), dma(4, 4),
        ],
        compiler_params=pltpu.CompilerParams(
            collective_id=0, has_side_effects=True, vmem_limit_bytes=VMEM_BYTES
        ),
        name="gather",
    )(nodes, w_qkv, w_out, grad_out, perm_row, blk)

    dkv, dqa = pl.pallas_call(
        attention_kernel,
        out_shape=(sds((128, QB, 128), BF), sds((16, QB, 128), BF)),
        in_specs=[pl.BlockSpec(memory_space=pltpu.SMEM), vm, vm],
        out_specs=(vm, vm),
        scratch_shapes=[pltpu.VMEM((1024, 128), BF), pltpu.VMEM((128, QB, 128), F32)],
        compiler_params=pltpu.CompilerParams(vmem_limit_bytes=VMEM_BYTES),
        name="attention",
    )(blk_all, kv_all.reshape(128, QB, 128), qg_all.reshape(16, QB, 128))

    return pl.pallas_call(
        scatter_kernel,
        out_shape=(sds((QB, 1024), BF), sds((QB, 1024), BF), sds((8, 1024), F32)),
        in_specs=[vm, vm, anywhere, anywhere, vm, vm],
        out_specs=(vm, vm, vm),
        scratch_shapes=[
            pltpu.VMEM((1024, 3072), BF),
            pltpu.VMEM((1024, 1024), BF),
            pltpu.VMEM((GROUP, GROUP), BF),
            pltpu.VMEM((SIDE, SIDE, GROUP, 128), BF),
            pltpu.VMEM((2 * SIDE, GROUP, 128), BF),
            pltpu.VMEM((SIDE, 2, GROUP, 128), BF),
            pltpu.VMEM((SIDE, 2, GROUP, 128), BF),
            pltpu.VMEM((SIDE, GROUP, 128), BF),
            pltpu.VMEM((GROUP, 512), BF),
            pltpu.VMEM((GROUP, 512), BF),
            pltpu.VMEM((GROUP, 512), BF),
            pltpu.VMEM((SIDE, QB, 512), BF),
            pltpu.VMEM((GROUP, 512), BF),
            pltpu.VMEM((SIDE, QB, 512), BF),
            pltpu.VMEM((QB, 1024), BF),
            pltpu.VMEM((QB, 3072), BF),
            pltpu.VMEM((16, 2, 32, 1024), F32),
            pltpu.VMEM((SIDE, QB, 1024), BF),
            pltpu.VMEM((SIDE, QB, 1024), BF),
            pltpu.VMEM((3, QB, 1024), BF),
            pltpu.VMEM((3, QB, 1024), BF),
            pltpu.VMEM((QB, 1024), BF),
            pltpu.VMEM((3, 32, 1024), BF),
            pltpu.VMEM((SIDE, 8, 1024), F32),
            pltpu.VMEM((3, 8, 1024), F32),
            dma(2), dma(2, 3), dma(2, 3), dma(2, 3), dma(2, 3),
            dma(4, 4), dma(4, 4), dma(4, 4), dma(4, 4), dma(10), dma(10),
        ],
        compiler_params=pltpu.CompilerParams(
            collective_id=1, has_side_effects=True, vmem_limit_bytes=VMEM_BYTES
        ),
        name="scatter",
    )(dkv.reshape(32, GROUP, 128), dqa.reshape(SIDE, GROUP, 128), w_qkv, w_out, grad_out, perm_row)


def solution(mesh):
    placed = (P(("seq", "blk"), None), P(), P(), P("seq"), P("seq", None), P(("seq", "blk"), None))
    return jax.shard_map(
        on_device,
        mesh=mesh,
        in_specs=placed,
        out_specs=(P(("seq", "blk"), None), P(("seq", "blk"), None), P(("seq", "blk"), None)),
        check_vma=False,
    )
```

```python
import jax
import jax.numpy as jnp
from jax import lax
from jax.experimental import pallas as pl
from jax.experimental.pallas import tpu as pltpu
from jax.sharding import PartitionSpec as P

HDIM = 64
QB = 128
GROUP = 512
SIDE = 4
BF = jnp.bfloat16
F32 = jnp.float32
MESH = pl.DeviceIdType.MESH
VMEM_BYTES = 56 * 1024 * 1024


def place():
    s = lax.axis_index("seq")
    z = lax.axis_index("blk")
    return s // 8, (s // 2) % 4, s % 2, z


def seq_of(x, y, c):
    return x * 8 + y * 2 + c


def turn(i, d):
    return lax.rem(i + (d + SIDE), SIDE)


def greet(x, y, c, z, y_steps):
    barrier = pltpu.get_barrier_semaphore()
    others = [(seq_of(x, y, c), turn(z, d)) for d in (1, 2, 3)]
    others += [(seq_of(turn(x, d), y, c), z) for d in (1, 2, 3)]
    others += [(seq_of(x, turn(y, d), c), z) for d in y_steps]
    others += [(seq_of(x, y, 1 - c), z)]
    for other in others:
        pl.semaphore_signal(barrier, inc=1, device_id=other, device_id_type=MESH)
    return lambda: pl.semaphore_wait(barrier, len(others))


def remote(src, dst, send_sem, recv_sem, device):
    return pltpu.make_async_remote_copy(
        src_ref=src,
        dst_ref=dst,
        send_sem=send_sem,
        recv_sem=recv_sem,
        device_id=device,
        device_id_type=MESH,
    )


def interleave(a, b):
    low = lax.broadcasted_iota(jnp.int32, a.shape, 1) < HDIM
    return (
        jnp.where(low, a, pltpu.roll(b, HDIM, 1)),
        jnp.where(low, pltpu.roll(a, HDIM, 1), b),
    )


def dot(a, b, ca=1, cb=0):
    return lax.dot_general(a, b, (((ca,), (cb,)), ((), ())), preferred_element_type=F32)


def store_pairs(ref, a, b):
    for half in range(2):
        cols = slice(128 * half, 128 * half + 128)
        first, second = interleave(a[:, cols], b[:, cols])
        ref[:, 256 * half : 256 * half + 128] = first.astype(BF)
        ref[:, 256 * half + 128 : 256 * half + 256] = second.astype(BF)


def gather_kernel(
    nodes, w_qkv, w_out, go, perm, blk, kv_all, qg_all, blk_all, go_all,
    wbuf, wobuf, pick, zs_kv, zr_kv, zs_qg, zr_qg, xs_kv, xs_qg,
    w_sem, zk_s, zk_r, zs_sem, zr_sem, xs_sem, xr_sem, ys_sem, yr_sem, cs_sem, cr_sem,
):
    x, y, c, z = place()
    group = seq_of(x, y, c)
    kv_cols = pl.ds(1024, 2048)
    load_kv = pltpu.make_async_copy(w_qkv.at[:, kv_cols], wbuf.at[:, kv_cols], w_sem.at[0])
    load_q = pltpu.make_async_copy(w_qkv.at[:, pl.ds(0, 1024)], wbuf.at[:, pl.ds(0, 1024)], w_sem.at[1])
    load_o = pltpu.make_async_copy(w_out, wobuf, w_sem.at[2])
    load_kv.start()
    load_q.start()
    load_o.start()
    ready = greet(x, y, c, z, (1, 3))
    own_rows = pl.ds(pl.multiple_of(z * QB, QB), QB)

    local = perm[...] - group * GROUP
    hits = lax.broadcasted_iota(jnp.int32, (GROUP, GROUP), 0) == local
    pick[...] = jnp.where(hits, 1.0, 0.0).T.astype(BF)

    def zk_copy(d, i):
        to, head = turn(z, d), turn(x, i)
        return remote(
            zs_kv.at[to, head], zr_kv.at[head, own_rows], zk_s.at[d - 1, i], zk_r.at[d - 1, i], (group, to)
        )

    def z_copy(which, d):
        to = turn(z, d)
        src = zs_qg.at[to] if which == 0 else go
        dst = (zr_qg, go_all)[which].at[own_rows]
        return remote(src, dst, zs_sem.at[which, d - 1], zr_sem.at[which, d - 1], (group, to))

    def project(first, second, put):
        for half in range(2):
            cols = slice(128 * half, 128 * half + 128)
            a, b = interleave(first[:, cols], second[:, cols])
            put(2 * half, a.astype(BF))
            put(2 * half + 1, b.astype(BF))

    load_kv.wait()
    for d in (2, 1, 3, 0):
        to = turn(z, d)
        off = pl.multiple_of(to * 256, 256)
        k = dot(nodes[...], wbuf[:, pl.ds(1024 + off, 256)])
        v = dot(nodes[...], wbuf[:, pl.ds(2048 + off, 256)])
        if d == 2:
            ready()
        if d:
            def put(h, val):
                zs_kv[to, h] = val
            project(k, v, put)
            zk_copy(d, 0).start()
        else:
            def put(h, val):
                zr_kv[h, own_rows] = val
            project(k, v, put)
    for i in (2, 1, 3):
        for d in (2, 1, 3):
            zk_copy(d, i).start()

    blk_copies = [
        remote(blk, blk_all.at[x], xs_sem.at[2, d - 1], xr_sem.at[2, d - 1], (seq_of(turn(x, d), y, c), z))
        for d in (1, 2, 3)
    ]
    for copy in blk_copies:
        copy.start()
    blk_all[x] = blk[...]

    def x_copy(which, d):
        to = turn(x, d)
        src = (xs_kv, xs_qg)[which].at[to]
        dst = kv_all.at[group] if which == 0 else qg_all.at[x]
        return remote(src, dst, xs_sem.at[which, d - 1], xr_sem.at[which, d - 1], (seq_of(to, y, c), z))

    def y_copy(d, k):
        mine = kv_all.at[seq_of(turn(x, -d), y, c)]
        to = seq_of(x, turn(y, (1, 3)[k]), c)
        return remote(mine, mine, ys_sem.at[d, k], yr_sem.at[d, k], (to, z))

    def relay(d, k):
        rows = pl.ds(256 * k, 256)
        step = (1, 3)[k]
        got = kv_all.at[seq_of(turn(x, -d), turn(y, -step), c), rows]
        return remote(got, got, ys_sem.at[d, 2 + k], yr_sem.at[d, 2 + k], (seq_of(x, turn(y, step), c), z))

    def cross(d, k):
        got = kv_all.at[seq_of(turn(x, -d), turn(y, -k), c)]
        return remote(got, got, cs_sem.at[d, k], cr_sem.at[d, k], (seq_of(x, y, 1 - c), z))

    def pass_on(d):
        y_copy(d, 0).start()
        y_copy(d, 1).start()
        cross(d, 0).start()

    load_q.wait()
    load_o.wait()
    for d in (2, 1, 3, 0):
        to = turn(z, d)
        off = pl.multiple_of(to * 256, 256)
        q = dot(nodes[...], wbuf[:, pl.ds(off, 256)])
        g = dot(go[...], wobuf[pl.ds(off, 256), :], 1, 1)
        if d:
            store_pairs(zs_qg.at[to], q, g)
        else:
            store_pairs(zr_qg.at[own_rows], q, g)
    go_all[own_rows] = go[...]

    for i in (0, 2, 1, 3):
        for d in (1, 2, 3):
            zk_copy(d, i).wait_recv()
        ordered = dot(pick[...], zr_kv[turn(x, i)]).astype(BF)
        if i:
            xs_kv[turn(x, i)] = ordered
            x_copy(0, i).start()
        else:
            kv_all[group] = ordered
            pass_on(0)
            for d in (2, 1, 3):
                z_copy(0, d).start()

    for d in (2, 1, 3):
        z_copy(1, d).start()

    x_copy(0, 2).wait_recv()
    pass_on(2)
    for d in (1, 2, 3):
        z_copy(0, d).wait_recv()
    ordered = dot(pick[...], zr_qg[...])
    for h in range(SIDE):
        xs_qg[h] = ordered[:, 128 * h : 128 * h + 128].astype(BF)
    for d in (2, 1, 3):
        x_copy(1, d).start()
    qg_all[x] = xs_qg[x]
    for d in (1, 3):
        x_copy(0, d).wait_recv()
        pass_on(d)

    for d in (0, 2, 1, 3):
        for k in range(2):
            y_copy(d, k).wait_recv()
            relay(d, k).start()
            cross(d, (1, 3)[k]).start()
    for d in (0, 2, 1, 3):
        relay(d, 0).wait_recv()
        relay(d, 1).wait_recv()
        cross(d, 2).start()

    for d in (1, 2, 3):
        x_copy(1, d).wait_recv()
        z_copy(1, d).wait_recv()
        blk_copies[d - 1].wait_recv()
    for d in range(SIDE):
        for k in range(SIDE):
            cross(d, k).wait_recv()
    for d in (1, 2, 3):
        for which in range(2):
            z_copy(which, d).wait_send()
            x_copy(which, d).wait_send()
        blk_copies[d - 1].wait_send()
        for i in range(SIDE):
            zk_copy(d, i).wait_send()
    for d in range(SIDE):
        for k in range(2):
            y_copy(d, k).wait_send()
            relay(d, k).wait_send()
        for k in range(SIDE):
            cross(d, k).wait_send()


def attention_kernel(listed, kv_all, qg_all, dkv_all, dqa_all, keys, acc):
    acc[...] = jnp.zeros_like(acc)
    low = lax.broadcasted_iota(jnp.int32, (QB, QB), 1) < HDIM
    top = lax.broadcasted_iota(jnp.int32, (QB, QB), 0) < HDIM
    scale = HDIM ** (-0.5)

    def softmax_and_grad(j, kept):
        ids = [listed[j // 4, j % 4, t] for t in range(8)]
        for t in range(8):
            kept[t * QB : (t + 1) * QB] = kv_all[ids[t]]
        qg = qg_all[j].astype(F32)
        both = jnp.concatenate([jnp.where(low, qg * scale, 0.0), jnp.where(low, 0.0, qg)], axis=0).astype(BF)
        rows = dot(kept[...], both, 1, 1)
        scores, grad_scores = rows[:, :QB], rows[:, QB:]
        raised = jnp.exp(scores - jnp.max(scores, axis=0, keepdims=True))
        probs = raised * (1.0 / jnp.sum(raised, axis=0, keepdims=True))
        delta = jnp.sum(probs * grad_scores, axis=0, keepdims=True)
        grad_logits = (probs * (grad_scores - delta)).astype(BF)
        return ids, both, jnp.concatenate([grad_logits, probs.astype(BF)], axis=1)

    def step(i, carry):
        parts_of = [softmax_and_grad(4 * i + u, keys.at[u]) for u in range(4)]
        for u, (ids, both, pair) in enumerate(parts_of):
            back = dot(keys[u], pair, 0, 0)
            dqa_all[4 * i + u] = jnp.where(top, back[:, :QB] * scale, back[:, QB:]).T.astype(BF)
            parts = dot(pair, both)
            for t in range(8):
                acc[ids[t]] += parts[t * QB : (t + 1) * QB]
        return carry

    lax.fori_loop(0, 4, step, 0)

    def finish(b, carry):
        dkv_all[b] = acc[b].astype(BF)
        return carry

    lax.fori_loop(0, 128, finish, 0, unroll=4)


def scatter_kernel(
    dkv, dqa, w_qkv, w_out, go_all, perm, out, grad_nodes, w_grad,
    wbuf, wobuf, place_hits, side, opp, y_recv, y_send, xs_kv, xr_kv, xr_qa, zs_kv, zr_kv, zs_qa, zr_qa,
    mixed, gproj, wpart, wc_send, wc_recv, wx_send, wx_recv, wy_send, wy_recv, wz_send, wz_recv,
    w_sem, zk_s, zk_r, zs_sem, zr_sem, xs_sem, xr_sem, ys_sem, yr_sem, cs_sem, cr_sem, ws_sem, wr_sem,
):
    x, y, c, z = place()
    group = seq_of(x, y, c)
    load_o = pltpu.make_async_copy(w_out, wobuf, w_sem.at[0])
    load_w = pltpu.make_async_copy(w_qkv, wbuf, w_sem.at[1])
    load_o.start()
    load_w.start()
    ready = greet(x, y, c, z, (1, 2, 3))
    sibling = (seq_of(x, y, 1 - c), z)
    own_rows = pl.ds(pl.multiple_of(z * QB, QB), QB)

    def cross(d, k):
        xt, yt = turn(x, d), turn(y, k)
        return remote(dkv.at[seq_of(xt, yt, 1 - c)], side.at[d, k], cs_sem.at[d, k], cr_sem.at[d, k], sibling)

    def x_copy(which, d):
        to = turn(x, d)
        src = xs_kv.at[to] if which == 0 else dqa.at[to]
        dst = (xr_kv, xr_qa)[which].at[x]
        return remote(src, dst, xs_sem.at[which, d - 1], xr_sem.at[which, d - 1], (seq_of(to, y, c), z))

    def zk_copy(d, i):
        to, head = turn(z, d), turn(x, i)
        rows = pl.ds(pl.multiple_of(to * QB, QB), QB)
        return remote(zs_kv.at[head, rows], zr_kv.at[z, head], zk_s.at[d - 1, i], zk_r.at[d - 1, i], (group, to))

    def zq_copy(d):
        to = turn(z, d)
        rows = pl.ds(pl.multiple_of(to * QB, QB), QB)
        return remote(zs_qa.at[rows], zr_qa.at[z], zs_sem.at[d - 1], zr_sem.at[d - 1], (group, to))

    def opposite(d, k):
        step = (1, 3)[k]
        rows = pl.ds(256 * k, 256)
        return remote(
            opp.at[d, rows], opp.at[SIDE + d, rows], ys_sem.at[d, k], yr_sem.at[d, k],
            (seq_of(x, turn(y, step), c), z),
        )

    def beside(d, k):
        step = (1, 3)[k]
        return remote(
            y_send.at[d, k], y_recv.at[d, k], ys_sem.at[d, 2 + k], yr_sem.at[d, 2 + k],
            (seq_of(x, turn(y, step), c), z),
        )

    def paired(d, k):
        cross(d, k).wait_recv()
        return dkv[seq_of(turn(x, d), turn(y, k), c)].astype(F32) + side[d, k].astype(F32)

    def to_neighbours(d):
        for k in range(2):
            total = paired(d, (1, 3)[k])
            opposite(d, k).wait_recv()
            rows = slice(256 * k, 256 * k + 256)
            rest = slice(256 - 256 * k, 512 - 256 * k)
            y_send[d, k, rows] = (total[rows] + opp[SIDE + d, rows].astype(F32)).astype(BF)
            y_send[d, k, rest] = total[rest].astype(BF)
            beside(d, k).start()

    def settle(d):
        for k in range(2):
            beside(d, k).wait_recv()
        total = paired(d, 0) + (y_recv[d, 0].astype(F32) + y_recv[d, 1].astype(F32))
        if d:
            xs_kv[turn(x, d)] = total.astype(BF)
            x_copy(0, d).start()
        else:
            xr_kv[x] = total.astype(BF)

    def w_x(d):
        return remote(
            wx_send.at[turn(x, d)], wx_recv.at[d - 1],
            ws_sem.at[d], wr_sem.at[d], (seq_of(turn(x, d), y, c), z),
        )

    def w_y(d):
        return remote(
            wy_send.at[turn(y, d)], wy_recv.at[d - 1],
            ws_sem.at[3 + d], wr_sem.at[3 + d], (seq_of(x, turn(y, d), c), z),
        )

    def w_z(d):
        return remote(
            wz_send.at[turn(z, d)], wz_recv.at[z], ws_sem.at[6 + d], wr_sem.at[6 + d], (group, turn(z, d))
        )

    order = (2, 1, 3, 0)
    ready()
    for k in (2, 1, 3, 0):
        for d in order:
            cross(d, k).start()
        if k == 2:
            for d in (2, 1, 3):
                x_copy(1, d).start()
    local = perm[...] - group * GROUP
    hits = lax.broadcasted_iota(jnp.int32, (GROUP, GROUP), 0) == local
    place_hits[...] = jnp.where(hits, 1.0, 0.0).astype(BF)
    xr_qa[x] = dqa[x]

    for d in order:
        opp[d] = paired(d, 2).astype(BF)
        opposite(d, 0).start()
        opposite(d, 1).start()
    to_neighbours(2)
    to_neighbours(1)

    for d in (1, 2, 3):
        x_copy(1, d).wait_recv()
    for h in range(SIDE):
        zs_qa[:, 128 * h : 128 * h + 128] = dot(place_hits[...], xr_qa[h]).astype(BF)
    for d in (2, 1, 3):
        zq_copy(d).start()
    zr_qa[z] = zs_qa[own_rows]
    to_neighbours(3)
    to_neighbours(0)

    group_mixed = []
    for half in range(2):
        a = zs_qa[:, 256 * half : 256 * half + 128].astype(F32)
        b = zs_qa[:, 256 * half + 128 : 256 * half + 256].astype(F32)
        group_mixed.append(interleave(a, b)[1].astype(BF))
    group_mixed = jnp.concatenate(group_mixed, axis=1)
    for i in range(SIDE):
        part = dot(go_all[:, 256 * i : 256 * i + 256], group_mixed, 0, 0)
        wpart[4 * i : 4 * i + 4] = part.reshape(4, 2, 32, 256)
    w_cross = remote(wc_send, wc_recv, ws_sem.at[0], wr_sem.at[0], sibling)
    wc_send[...] = wpart[:, 1 - c].astype(BF)
    w_cross.start()

    settle(2)

    for d in (1, 2, 3):
        zq_copy(d).wait_recv()
    for h in range(SIDE):
        for half in range(2):
            a = zr_qa[h, :, 256 * half : 256 * half + 128].astype(F32)
            b = zr_qa[h, :, 256 * half + 128 : 256 * half + 256].astype(F32)
            cols = slice(256 * h + 128 * half, 256 * h + 128 * half + 128)
            first, second = interleave(a, b)
            gproj[:, cols] = first.astype(BF)
            mixed[:, cols] = second.astype(BF)
    load_o.wait()
    out[...] = dot(mixed[...], wobuf[...]).astype(BF)

    settle(1)
    w_cross.wait_recv()
    wsum = (wpart[:, c] + wc_recv[...].astype(F32)).reshape(SIDE, QB, 256)
    wx_send[...] = wsum.astype(BF)
    for d in (2, 1, 3):
        w_x(d).start()
    settle(3)

    def settle_z(i):
        head = turn(x, i)
        if i:
            x_copy(0, SIDE - i).wait_recv()
        zs_kv[head] = dot(place_hits[...], xr_kv[head]).astype(BF)
        for d in (2, 1, 3):
            zk_copy(d, i).start()
        zr_kv[z, head] = zs_kv[head, own_rows]

    settle_z(2)
    wrows = wx_send[x].astype(F32)
    for d in (1, 2, 3):
        w_x(d).wait_recv()
        wrows += wx_recv[d - 1].astype(F32)
    wy_send[...] = wrows.reshape(SIDE, 32, 256)
    for d in (2, 1, 3):
        w_y(d).start()
    settle_z(3)
    settle(0)
    settle_z(0)
    settle_z(1)

    wrows = wy_send[y]
    for d in (1, 2, 3):
        w_y(d).wait_recv()
        wrows += wy_recv[d - 1]
    wz_send[...] = wrows.reshape(SIDE, 8, 256)
    for d in (2, 1, 3):
        w_z(d).start()
    wz_recv[z] = wz_send[z]

    for i in (2, 3, 0, 1):
        for d in (1, 2, 3):
            remote(
                zs_kv.at[turn(x, i), own_rows], zr_kv.at[turn(z, -d), turn(x, i)],
                zk_s.at[d - 1, i], zk_r.at[d - 1, i], (group, turn(z, -d)),
            ).wait_recv()
    for h in range(SIDE):
        for half in range(2):
            a = zr_kv[h, 2 * half].astype(F32)
            b = zr_kv[h, 2 * half + 1].astype(F32)
            col = 256 * h + 128 * half
            first, second = interleave(a, b)
            gproj[:, 1024 + col : 1024 + col + 128] = first.astype(BF)
            gproj[:, 2048 + col : 2048 + col + 128] = second.astype(BF)
    load_w.wait()
    for i in range(SIDE):
        rows = slice(256 * i, 256 * i + 256)
        grad_nodes[:, rows] = dot(gproj[...], wbuf[rows, :], 1, 1).astype(BF)

    for d in (1, 2, 3):
        w_z(d).wait_recv()
    for h in range(SIDE):
        w_grad[:, 256 * h : 256 * h + 256] = wz_recv[h]

    w_cross.wait_send()
    for d in (1, 2, 3):
        for which in range(2):
            x_copy(which, d).wait_send()
        zq_copy(d).wait_send()
        w_z(d).wait_send()
        w_x(d).wait_send()
        w_y(d).wait_send()
        for i in range(SIDE):
            zk_copy(d, i).wait_send()
    for d in range(SIDE):
        for k in range(SIDE):
            cross(d, k).wait_send()
        for k in range(2):
            opposite(d, k).wait_send()
            beside(d, k).wait_send()


def hand_on(*refs):
    half = len(refs) // 2
    for i in range(half):
        refs[half + i][...] = refs[i][...]


def dma(*shape):
    return pltpu.SemaphoreType.DMA(shape)


def on_device(nodes, w_qkv, w_out, perm, blocks, grad_out):
    vm = pl.BlockSpec(memory_space=pltpu.VMEM)
    anywhere = pl.BlockSpec(memory_space=pl.ANY)
    sds = jax.ShapeDtypeStruct
    perm_row = perm.reshape(1, GROUP)
    blk = jnp.pad(blocks, ((0, 4), (0, 120)))
    kv_all, qg_all, blk_all, go_all = pl.pallas_call(
        gather_kernel,
        out_shape=(
            sds((32, GROUP, 128), BF),
            sds((SIDE, GROUP, 128), BF),
            sds((SIDE, 8, 128), jnp.int32),
            sds((GROUP, 1024), BF),
        ),
        in_specs=[vm, anywhere, anywhere, vm, vm, vm],
        out_specs=(vm, vm, vm, vm),
        scratch_shapes=[
            pltpu.VMEM((1024, 3072), BF),
            pltpu.VMEM((1024, 1024), BF),
            pltpu.VMEM((GROUP, GROUP), BF),
            pltpu.VMEM((SIDE, SIDE, QB, 128), BF),
            pltpu.VMEM((SIDE, GROUP, 128), BF),
            pltpu.VMEM((SIDE, QB, 512), BF),
            pltpu.VMEM((GROUP, 512), BF),
            pltpu.VMEM((SIDE, GROUP, 128), BF),
            pltpu.VMEM((SIDE, GROUP, 128), BF),
            dma(3), dma(3, 4), dma(3, 4), dma(2, 3), dma(2, 3), dma(3, 3), dma(3, 3),
            dma(4, 4), dma(4, 4), dma(4, 4), dma(4, 4),
        ],
        compiler_params=pltpu.CompilerParams(
            collective_id=0, has_side_effects=True, vmem_limit_bytes=VMEM_BYTES
        ),
        name="gather",
    )(nodes, w_qkv, w_out, grad_out, perm_row, blk)

    dkv, dqa = pl.pallas_call(
        attention_kernel,
        out_shape=(sds((128, QB, 128), BF), sds((16, QB, 128), BF)),
        in_specs=[pl.BlockSpec(memory_space=pltpu.SMEM), vm, vm],
        out_specs=(vm, vm),
        scratch_shapes=[pltpu.VMEM((4, 1024, 128), BF), pltpu.VMEM((128, QB, 128), F32)],
        compiler_params=pltpu.CompilerParams(vmem_limit_bytes=VMEM_BYTES),
        name="attention",
    )(blk_all, kv_all.reshape(128, QB, 128), qg_all.reshape(16, QB, 128))

    shapes = (sds((QB, 1024), BF), sds((QB, 1024), BF), sds((8, 1024), F32))
    results = pl.pallas_call(
        scatter_kernel,
        out_shape=shapes,
        in_specs=[vm, vm, anywhere, anywhere, vm, vm],
        out_specs=(vm, vm, vm),
        scratch_shapes=[
            pltpu.VMEM((1024, 3072), BF),
            pltpu.VMEM((1024, 1024), BF),
            pltpu.VMEM((GROUP, GROUP), BF),
            pltpu.VMEM((SIDE, SIDE, GROUP, 128), BF),
            pltpu.VMEM((2 * SIDE, GROUP, 128), BF),
            pltpu.VMEM((SIDE, 2, GROUP, 128), BF),
            pltpu.VMEM((SIDE, 2, GROUP, 128), BF),
            pltpu.VMEM((SIDE, GROUP, 128), BF),
            pltpu.VMEM((SIDE, GROUP, 128), BF),
            pltpu.VMEM((SIDE, GROUP, 128), BF),
            pltpu.VMEM((SIDE, GROUP, 128), BF),
            pltpu.VMEM((SIDE, SIDE, QB, 128), BF),
            pltpu.VMEM((GROUP, 512), BF),
            pltpu.VMEM((SIDE, QB, 512), BF),
            pltpu.VMEM((QB, 1024), BF),
            pltpu.VMEM((QB, 3072), BF),
            pltpu.VMEM((16, 2, 32, 256), F32),
            pltpu.VMEM((16, 32, 256), BF),
            pltpu.VMEM((16, 32, 256), BF),
            pltpu.VMEM((SIDE, QB, 256), BF),
            pltpu.VMEM((3, QB, 256), BF),
            pltpu.VMEM((SIDE, 32, 256), F32),
            pltpu.VMEM((3, 32, 256), F32),
            pltpu.VMEM((SIDE, 8, 256), F32),
            pltpu.VMEM((SIDE, 8, 256), F32),
            dma(2), dma(3, 4), dma(3, 4), dma(3), dma(3), dma(2, 3), dma(2, 3),
            dma(4, 4), dma(4, 4), dma(4, 4), dma(4, 4), dma(10), dma(10),
        ],
        compiler_params=pltpu.CompilerParams(
            collective_id=1, has_side_effects=True, vmem_limit_bytes=VMEM_BYTES
        ),
        name="scatter",
    )(dkv.reshape(32, GROUP, 128), dqa.reshape(SIDE, GROUP, 128), w_qkv, w_out, go_all, perm_row)
    return pl.pallas_call(
        hand_on,
        out_shape=shapes,
        in_specs=[vm] * 3,
        out_specs=(vm,) * 3,
        name="results",
    )(*results)


def solution(mesh):
    placed = (P(("seq", "blk"), None), P(), P(), P("seq"), P("seq", None), P(("seq", "blk"), None))
    return jax.shard_map(
        on_device,
        mesh=mesh,
        in_specs=placed,
        out_specs=(P(("seq", "blk"), None), P(("seq", "blk"), None), P(("seq", "blk"), None)),
        check_vma=False,
    )
```

```python
import jax
import jax.numpy as jnp
from jax import lax
from jax.experimental import pallas as pl
from jax.experimental.pallas import tpu as pltpu
from jax.sharding import PartitionSpec as P

HDIM = 64
QB = 128
GROUP = 512
SIDE = 4
BF = jnp.bfloat16
F32 = jnp.float32
MESH = pl.DeviceIdType.MESH
VMEM_BYTES = 56 * 1024 * 1024


def place():
    s = lax.axis_index("seq")
    z = lax.axis_index("blk")
    return s // 8, (s // 2) % 4, s % 2, z


def seq_of(x, y, c):
    return x * 8 + y * 2 + c


def turn(i, d):
    return lax.rem(i + (d + SIDE), SIDE)


def greet(x, y, c, z, y_steps):
    barrier = pltpu.get_barrier_semaphore()
    others = [(seq_of(x, y, c), turn(z, d)) for d in (1, 2, 3)]
    others += [(seq_of(turn(x, d), y, c), z) for d in (1, 2, 3)]
    others += [(seq_of(x, turn(y, d), c), z) for d in y_steps]
    others += [(seq_of(x, y, 1 - c), z)]
    for other in others:
        pl.semaphore_signal(barrier, inc=1, device_id=other, device_id_type=MESH)
    return lambda: pl.semaphore_wait(barrier, len(others))


def remote(src, dst, send_sem, recv_sem, device):
    return pltpu.make_async_remote_copy(
        src_ref=src,
        dst_ref=dst,
        send_sem=send_sem,
        recv_sem=recv_sem,
        device_id=device,
        device_id_type=MESH,
    )


def interleave(a, b):
    low = lax.broadcasted_iota(jnp.int32, a.shape, 1) < HDIM
    return (
        jnp.where(low, a, pltpu.roll(b, HDIM, 1)),
        jnp.where(low, pltpu.roll(a, HDIM, 1), b),
    )


def dot(a, b, ca=1, cb=0):
    return lax.dot_general(a, b, (((ca,), (cb,)), ((), ())), preferred_element_type=F32)


def store_pairs(ref, a, b):
    for half in range(2):
        cols = slice(128 * half, 128 * half + 128)
        first, second = interleave(a[:, cols], b[:, cols])
        ref[:, 256 * half : 256 * half + 128] = first.astype(BF)
        ref[:, 256 * half + 128 : 256 * half + 256] = second.astype(BF)


def plan_sums(blk_all, plan):
    shape = (QB, QB)
    lane = lax.broadcasted_iota(jnp.int32, (1, QB), 1)
    flat = jnp.zeros((1, QB), jnp.int32)
    for j in range(16):
        row = jnp.where(lane < 8, blk_all[j // 4, j % 4 : j % 4 + 1, :], 0)
        flat += pltpu.roll(row, 8 * j, 1) if j else row
    down = lax.broadcasted_iota(jnp.int32, shape, 0)
    across = lax.broadcasted_iota(jnp.int32, shape, 1)
    by_lane = jnp.broadcast_to(flat, shape)
    by_row = by_lane.T

    def total(values):
        return jnp.sum(values, axis=0, keepdims=True)

    def count(hits):
        return total(jnp.where(hits, 1, 0))

    rank = count((by_row < by_lane) | ((by_row == by_lane) & (down < across)))
    hits = jnp.broadcast_to(rank, shape).T == across
    order = total(jnp.where(hits, down, 0))
    sorted_ids = total(jnp.where(hits, by_row, 0))
    goes_on = jnp.where((sorted_ids == pltpu.roll(sorted_ids, 1, 1)) & (lane > 0), 1, 0)
    last = jnp.maximum(count(by_row <= across) - 1, 0)
    some = jnp.minimum(count(by_row == across), 1)
    plan[...] = jnp.concatenate([order, goes_on, last, some, jnp.zeros((4, QB), jnp.int32)], axis=0)


def sublayer_kernel(
    nodes_in, w_qkv, w_out, go_in, perm, blk, out, grad_nodes, w_grad,
    nodes, go, wbuf, wobuf, pick, place_hits,
    zs_kv, zr_kv, zs_qg, zr_qg, xs_kv, xs_qg, kv_all, qg_all, blk_all, go_all,
    plan, plan_s, listed, keys, parts, seg, dqa,
    dkv, side, opp, y_recv, y_send, bxs_kv, bxr_kv, bxr_qa, bzs_kv, bzr_kv, bzs_qa, bzr_qa,
    mixed, gproj, wpart, wc_send, wc_recv, wx_send, wx_recv, wy_send, wy_recv, wz_send, wz_recv,
    w_sem, zk_s, zk_r, zs_sem, zr_sem, xs_sem, xr_sem, ys_sem, yr_sem, cs_sem, cr_sem,
    bzk_s, bzk_r, bzs_sem, bzr_sem, bxs_sem, bxr_sem, bys_sem, byr_sem, bcs_sem, bcr_sem, ws_sem, wr_sem,
):
    x, y, c, z = place()
    group = seq_of(x, y, c)
    sibling = (seq_of(x, y, 1 - c), z)
    order = (2, 1, 3, 0)
    kv_cols = pl.ds(1024, 2048)
    loads = [
        pltpu.make_async_copy(src, dst, w_sem.at[i])
        for i, (src, dst) in enumerate((
            (nodes_in, nodes),
            (w_qkv.at[:, kv_cols], wbuf.at[:, kv_cols]),
            (w_qkv.at[:, pl.ds(0, 1024)], wbuf.at[:, pl.ds(0, 1024)]),
            (go_in, go),
            (w_out, wobuf),
        ))
    ]
    for load in loads:
        load.start()
    ready = greet(x, y, c, z, (1, 2, 3))
    own_rows = pl.ds(pl.multiple_of(z * QB, QB), QB)

    local = perm[...] - group * GROUP
    hits = lax.broadcasted_iota(jnp.int32, (GROUP, GROUP), 0) == local
    one_hot = jnp.where(hits, 1.0, 0.0)
    pick[...] = one_hot.T.astype(BF)
    place_hits[...] = one_hot.astype(BF)

    def zk_copy(d, i):
        to, head = turn(z, d), turn(x, i)
        return remote(
            zs_kv.at[to, head], zr_kv.at[head, own_rows], zk_s.at[d - 1, i], zk_r.at[d - 1, i], (group, to)
        )

    def z_copy(which, d):
        to = turn(z, d)
        src = zs_qg.at[to] if which == 0 else go
        dst = (zr_qg, go_all)[which].at[own_rows]
        return remote(src, dst, zs_sem.at[which, d - 1], zr_sem.at[which, d - 1], (group, to))

    def project(first, second, put):
        for half in range(2):
            cols = slice(128 * half, 128 * half + 128)
            a, b = interleave(first[:, cols], second[:, cols])
            put(2 * half, a.astype(BF))
            put(2 * half + 1, b.astype(BF))

    def group_rows(g):
        return kv_all.at[pl.ds(pl.multiple_of(4 * g, 4), 4)]

    def x_copy(which, d):
        to = turn(x, d)
        src = (xs_kv, xs_qg)[which].at[to]
        dst = group_rows(group) if which == 0 else qg_all.at[x]
        return remote(src, dst, xs_sem.at[which, d - 1], xr_sem.at[which, d - 1], (seq_of(to, y, c), z))

    def y_copy(d, k):
        mine = group_rows(seq_of(turn(x, -d), y, c))
        to = seq_of(x, turn(y, (1, 3)[k]), c)
        return remote(mine, mine, ys_sem.at[d, k], yr_sem.at[d, k], (to, z))

    def relay(d, k):
        step = (1, 3)[k]
        first = pl.multiple_of(4 * seq_of(turn(x, -d), turn(y, -step), c) + 2 * k, 2)
        got = kv_all.at[pl.ds(first, 2)]
        return remote(got, got, ys_sem.at[d, 2 + k], yr_sem.at[d, 2 + k], (seq_of(x, turn(y, step), c), z))

    def cross(d, k):
        got = group_rows(seq_of(turn(x, -d), turn(y, -k), c))
        return remote(got, got, cs_sem.at[d, k], cr_sem.at[d, k], sibling)

    def pass_on(d):
        y_copy(d, 0).start()
        y_copy(d, 1).start()
        cross(d, 0).start()

    def relay_on(d):
        for k in range(2):
            y_copy(d, k).wait_recv()
            relay(d, k).start()
            cross(d, (1, 3)[k]).start()

    loads[0].wait()
    loads[1].wait()
    for d in (2, 1, 3, 0):
        to = turn(z, d)
        off = pl.multiple_of(to * 256, 256)
        k = dot(nodes[...], wbuf[:, pl.ds(1024 + off, 256)])
        v = dot(nodes[...], wbuf[:, pl.ds(2048 + off, 256)])
        if d == 2:
            ready()
        if d:
            def put(h, val):
                zs_kv[to, h] = val
            project(k, v, put)
            zk_copy(d, 0).start()
        else:
            def put(h, val):
                zr_kv[h, own_rows] = val
            project(k, v, put)
    for i in (2, 1, 3):
        for d in (2, 1, 3):
            zk_copy(d, i).start()

    blk_copies = [
        remote(blk, blk_all.at[x], xs_sem.at[2, d - 1], xr_sem.at[2, d - 1], (seq_of(turn(x, d), y, c), z))
        for d in (1, 2, 3)
    ]
    for copy in blk_copies:
        copy.start()
    blk_all[x] = blk[...]

    for load in loads[2:]:
        load.wait()
    for d in (2, 1, 3, 0):
        to = turn(z, d)
        off = pl.multiple_of(to * 256, 256)
        q = dot(nodes[...], wbuf[:, pl.ds(off, 256)])
        g = dot(go[...], wobuf[pl.ds(off, 256), :], 1, 1)
        if d:
            store_pairs(zs_qg.at[to], q, g)
        else:
            store_pairs(zr_qg.at[own_rows], q, g)
    go_all[own_rows] = go[...]

    for i in (0, 2, 1, 3):
        for d in (1, 2, 3):
            zk_copy(d, i).wait_recv()
        ordered = dot(pick[...], zr_kv[turn(x, i)]).astype(BF)
        if i:
            xs_kv[turn(x, i)] = ordered.reshape(4, QB, 128)
            x_copy(0, i).start()
        else:
            kv_all[pl.ds(pl.multiple_of(4 * group, 4), 4)] = ordered.reshape(4, QB, 128)
            pass_on(0)
            for d in (2, 1, 3):
                z_copy(0, d).start()

    relay_on(0)
    x_copy(0, 2).wait_recv()
    pass_on(2)
    for d in (1, 2, 3):
        z_copy(0, d).wait_recv()
    ordered = dot(pick[...], zr_qg[...])
    for h in range(SIDE):
        xs_qg[h] = ordered[:, 128 * h : 128 * h + 128].astype(BF)
    for d in (2, 1, 3):
        x_copy(1, d).start()
    for d in (2, 1, 3):
        z_copy(1, d).start()
    qg_all[x] = xs_qg[x]
    for d in (1, 3):
        x_copy(0, d).wait_recv()
        pass_on(d)
    relay_on(2)

    for d in (1, 2, 3):
        blk_copies[d - 1].wait_recv()
    plan_sums(blk_all, plan)
    plan_copy = pltpu.make_async_copy(plan, plan_s, w_sem.at[5])
    listed_copy = pltpu.make_async_copy(blk_all, listed, w_sem.at[6])
    plan_copy.start()
    listed_copy.start()

    relay_on(1)
    relay_on(3)
    for d in (0, 2, 1, 3):
        relay(d, 0).wait_recv()
        relay(d, 1).wait_recv()
        cross(d, 2).start()
    for d in (1, 2, 3):
        x_copy(1, d).wait_recv()
    plan_copy.wait()
    listed_copy.wait()
    for d in range(SIDE):
        for k in range(SIDE):
            cross(d, k).wait_recv()

    low = lax.broadcasted_iota(jnp.int32, (QB, QB), 1) < HDIM
    top = lax.broadcasted_iota(jnp.int32, (QB, QB), 0) < HDIM
    scale = HDIM ** (-0.5)

    def softmax_and_grad(i, u, kept):
        for t in range(8):
            kept[t * QB : (t + 1) * QB] = kv_all[listed[i, u, t]]
        qg = qg_all[i, u * QB : (u + 1) * QB].astype(F32)
        both = jnp.concatenate([jnp.where(low, qg * scale, 0.0), jnp.where(low, 0.0, qg)], axis=0).astype(BF)
        rows = dot(kept[...], both, 1, 1)
        scores, grad_scores = rows[:, :QB], rows[:, QB:]
        raised = jnp.exp(scores - jnp.max(scores, axis=0, keepdims=True))
        probs = raised * (1.0 / jnp.sum(raised, axis=0, keepdims=True))
        delta = jnp.sum(probs * grad_scores, axis=0, keepdims=True)
        grad_logits = (probs * (grad_scores - delta)).astype(BF)
        return both, jnp.concatenate([grad_logits, probs.astype(BF)], axis=1)

    def bx_qa(d):
        to = turn(x, d)
        return remote(
            dqa.at[to], bxr_qa.at[x], bxs_sem.at[1, d - 1], bxr_sem.at[1, d - 1], (seq_of(to, y, c), z)
        )

    def step(i, carry):
        pairs = [softmax_and_grad(i, u, keys.at[u]) for u in range(4)]
        for u, (both, pair) in enumerate(pairs):
            back = dot(keys[u], pair, 0, 0)
            dqa[i, u * QB : (u + 1) * QB] = jnp.where(top, back[:, :QB] * scale, back[:, QB:]).T.astype(BF)
            made = dot(pair, both).astype(BF)
            parts[pl.ds(pl.multiple_of(32 * i + 8 * u, 8), 8)] = made.reshape(8, QB, 128)
        return carry

    lax.fori_loop(0, 4, step, 0)
    for d in (2, 1, 3):
        bx_qa(d).start()
    bxr_qa[x] = dqa[x]

    def add_entry(i, run):
        run = run * plan_s[1, i].astype(F32) + parts[jnp.clip(plan_s[0, i], 0, QB - 1)].astype(F32)
        seg[i] = run
        return run

    lax.fori_loop(0, QB, add_entry, jnp.zeros((QB, 128), F32), unroll=4)

    def partial_sum(g, n):
        b = 4 * g + n
        return seg[jnp.clip(plan_s[2, b], 0, QB - 1)] * plan_s[3, b].astype(F32)

    def bcross(d, k):
        return remote(dkv.at[d, k], side.at[d, k], bcs_sem.at[d, k], bcr_sem.at[d, k], sibling)

    def bx_kv(d):
        to = turn(x, d)
        return remote(
            bxs_kv.at[to], bxr_kv.at[x], bxs_sem.at[0, d - 1], bxr_sem.at[0, d - 1], (seq_of(to, y, c), z)
        )

    def bzk_copy(d, i):
        to, head = turn(z, d), turn(x, i)
        rows = pl.ds(pl.multiple_of(to * QB, QB), QB)
        return remote(bzs_kv.at[head, rows], bzr_kv.at[z, head], bzk_s.at[d - 1, i], bzk_r.at[d - 1, i], (group, to))

    def bzq_copy(d):
        to = turn(z, d)
        rows = pl.ds(pl.multiple_of(to * QB, QB), QB)
        return remote(bzs_qa.at[rows], bzr_qa.at[z], bzs_sem.at[d - 1], bzr_sem.at[d - 1], (group, to))

    def opposite(d, k):
        half = pl.ds(2 * k, 2)
        return remote(
            opp.at[d, half], opp.at[SIDE + d, half], bys_sem.at[d, k], byr_sem.at[d, k],
            (seq_of(x, turn(y, (1, 3)[k]), c), z),
        )

    def beside(d, k):
        return remote(
            y_send.at[d, k], y_recv.at[d, k], bys_sem.at[d, 2 + k], byr_sem.at[d, 2 + k],
            (seq_of(x, turn(y, (1, 3)[k]), c), z),
        )

    def paired(d, k, n):
        return partial_sum(seq_of(turn(x, d), turn(y, k), c), n) + side[d, k, n].astype(F32)

    def to_opposite(d):
        bcross(d, 2).wait_recv()
        for n in range(4):
            opp[d, n] = paired(d, 2, n).astype(BF)
        opposite(d, 0).start()
        opposite(d, 1).start()

    def to_neighbours(d):
        for k in range(2):
            bcross(d, (1, 3)[k]).wait_recv()
            opposite(d, k).wait_recv()
            for n in range(4):
                total = paired(d, (1, 3)[k], n)
                if n // 2 == k:
                    total += opp[SIDE + d, n].astype(F32)
                y_send[d, k, n] = total.astype(BF)
            beside(d, k).start()

    def settle(d):
        bcross(d, 0).wait_recv()
        for k in range(2):
            beside(d, k).wait_recv()
        for n in range(4):
            total = paired(d, 0, n) + (y_recv[d, 0, n].astype(F32) + y_recv[d, 1, n].astype(F32))
            rows = slice(QB * n, QB * n + QB)
            if d:
                bxs_kv[turn(x, d), rows] = total.astype(BF)
            else:
                bxr_kv[x, rows] = total.astype(BF)
        if d:
            bx_kv(d).start()

    def settle_z(i):
        head = turn(x, i)
        if i:
            bx_kv(SIDE - i).wait_recv()
        bzs_kv[head] = dot(place_hits[...], bxr_kv[head]).astype(BF)
        for d in (2, 1, 3):
            bzk_copy(d, i).start()
        bzr_kv[z, head] = bzs_kv[head, own_rows]

    def w_x(d):
        return remote(
            wx_send.at[turn(x, d)], wx_recv.at[d - 1],
            ws_sem.at[d], wr_sem.at[d], (seq_of(turn(x, d), y, c), z),
        )

    def w_y(d):
        return remote(
            wy_send.at[turn(y, d)], wy_recv.at[d - 1],
            ws_sem.at[3 + d], wr_sem.at[3 + d], (seq_of(x, turn(y, d), c), z),
        )

    def w_z(d):
        return remote(
            wz_send.at[turn(z, d)], wz_recv.at[z], ws_sem.at[6 + d], wr_sem.at[6 + d], (group, turn(z, d))
        )

    for k in (2, 1, 3, 0):
        for d in order:
            for n in range(4):
                dkv[d, k, n] = partial_sum(seq_of(turn(x, d), turn(y, k), 1 - c), n).astype(BF)
            bcross(d, k).start()
    for d in order:
        to_opposite(d)
    to_neighbours(2)
    to_neighbours(1)

    for d in (1, 2, 3):
        bx_qa(d).wait_recv()
    for h in range(SIDE):
        bzs_qa[:, 128 * h : 128 * h + 128] = dot(place_hits[...], bxr_qa[h]).astype(BF)
    for d in (2, 1, 3):
        bzq_copy(d).start()
    bzr_qa[z] = bzs_qa[own_rows]
    to_neighbours(3)
    to_neighbours(0)

    for d in (1, 2, 3):
        z_copy(1, d).wait_recv()
    group_mixed = []
    for half in range(2):
        a = bzs_qa[:, 256 * half : 256 * half + 128].astype(F32)
        b = bzs_qa[:, 256 * half + 128 : 256 * half + 256].astype(F32)
        group_mixed.append(interleave(a, b)[1].astype(BF))
    group_mixed = jnp.concatenate(group_mixed, axis=1)
    for i in range(SIDE):
        part = dot(go_all[:, 256 * i : 256 * i + 256], group_mixed, 0, 0)
        wpart[4 * i : 4 * i + 4] = part.reshape(4, 2, 32, 256)
    w_cross = remote(wc_send, wc_recv, ws_sem.at[0], wr_sem.at[0], sibling)
    wc_send[...] = wpart[:, 1 - c].astype(BF)
    w_cross.start()

    settle(2)

    for d in (1, 2, 3):
        bzq_copy(d).wait_recv()
    for h in range(SIDE):
        for half in range(2):
            a = bzr_qa[h, :, 256 * half : 256 * half + 128].astype(F32)
            b = bzr_qa[h, :, 256 * half + 128 : 256 * half + 256].astype(F32)
            cols = slice(256 * h + 128 * half, 256 * h + 128 * half + 128)
            first, second = interleave(a, b)
            gproj[:, cols] = first.astype(BF)
            mixed[:, cols] = second.astype(BF)
    out[...] = dot(mixed[...], wobuf[...]).astype(BF)

    settle(1)
    w_cross.wait_recv()
    wsum = (wpart[:, c] + wc_recv[...].astype(F32)).reshape(SIDE, QB, 256)
    wx_send[...] = wsum.astype(BF)
    for d in (2, 1, 3):
        w_x(d).start()
    settle(3)

    settle_z(2)
    wrows = wx_send[x].astype(F32)
    for d in (1, 2, 3):
        w_x(d).wait_recv()
        wrows += wx_recv[d - 1].astype(F32)
    wy_send[...] = wrows.reshape(SIDE, 32, 256)
    for d in (2, 1, 3):
        w_y(d).start()
    settle_z(3)
    settle(0)
    settle_z(0)
    settle_z(1)

    wrows = wy_send[y]
    for d in (1, 2, 3):
        w_y(d).wait_recv()
        wrows += wy_recv[d - 1]
    wz_send[...] = wrows.reshape(SIDE, 8, 256)
    for d in (2, 1, 3):
        w_z(d).start()
    wz_recv[z] = wz_send[z]

    for i in (2, 3, 0, 1):
        for d in (1, 2, 3):
            remote(
                bzs_kv.at[turn(x, i), own_rows], bzr_kv.at[turn(z, -d), turn(x, i)],
                bzk_s.at[d - 1, i], bzk_r.at[d - 1, i], (group, turn(z, -d)),
            ).wait_recv()
    for h in range(SIDE):
        for half in range(2):
            a = bzr_kv[h, 2 * half].astype(F32)
            b = bzr_kv[h, 2 * half + 1].astype(F32)
            col = 256 * h + 128 * half
            first, second = interleave(a, b)
            gproj[:, 1024 + col : 1024 + col + 128] = first.astype(BF)
            gproj[:, 2048 + col : 2048 + col + 128] = second.astype(BF)
    for i in range(SIDE):
        rows = slice(256 * i, 256 * i + 256)
        grad_nodes[:, rows] = dot(gproj[...], wbuf[rows, :], 1, 1).astype(BF)

    for d in (1, 2, 3):
        w_z(d).wait_recv()
    for h in range(SIDE):
        w_grad[:, 256 * h : 256 * h + 256] = wz_recv[h]

    w_cross.wait_send()
    for d in (1, 2, 3):
        for which in range(2):
            z_copy(which, d).wait_send()
            x_copy(which, d).wait_send()
        blk_copies[d - 1].wait_send()
        bx_kv(d).wait_send()
        bx_qa(d).wait_send()
        bzq_copy(d).wait_send()
        w_z(d).wait_send()
        w_x(d).wait_send()
        w_y(d).wait_send()
        for i in range(SIDE):
            zk_copy(d, i).wait_send()
            bzk_copy(d, i).wait_send()
    for d in range(SIDE):
        for k in range(2):
            y_copy(d, k).wait_send()
            relay(d, k).wait_send()
            opposite(d, k).wait_send()
            beside(d, k).wait_send()
        for k in range(SIDE):
            cross(d, k).wait_send()
            bcross(d, k).wait_send()


def hand_on(*refs):
    half = len(refs) // 2
    for i in range(half):
        refs[half + i][...] = refs[i][...]


def dma(*shape):
    return pltpu.SemaphoreType.DMA(shape)


def low_precision(*shape):
    return pltpu.VMEM(shape, BF)


def full(*shape):
    return pltpu.VMEM(shape, F32)


def on_device(nodes, w_qkv, w_out, perm, blocks, grad_out):
    vm = pl.BlockSpec(memory_space=pltpu.VMEM)
    anywhere = pl.BlockSpec(memory_space=pl.ANY)
    sds = jax.ShapeDtypeStruct
    shapes = (sds((QB, 1024), BF), sds((QB, 1024), BF), sds((8, 1024), F32))
    low = low_precision
    heads = (SIDE, GROUP, 128)
    results = pl.pallas_call(
        sublayer_kernel,
        out_shape=shapes,
        in_specs=[anywhere, anywhere, anywhere, anywhere, vm, vm],
        out_specs=(vm, vm, vm),
        scratch_shapes=[
            low(QB, 1024), low(QB, 1024), low(1024, 3072), low(1024, 1024), low(GROUP, GROUP), low(GROUP, GROUP),
            low(SIDE, SIDE, QB, 128), low(*heads), low(SIDE, QB, 512), low(GROUP, 512),
            low(SIDE, 4, QB, 128), low(*heads), low(QB, QB, 128), low(*heads),
            pltpu.VMEM((SIDE, 8, 128), jnp.int32), low(GROUP, 1024),
            pltpu.VMEM((8, QB), jnp.int32), pltpu.SMEM((8, QB), jnp.int32), pltpu.SMEM((SIDE, 8, 128), jnp.int32),
            low(4, 1024, 128), low(QB, QB, 128), full(QB, QB, 128), low(*heads),
            low(SIDE, SIDE, 4, QB, 128), low(SIDE, SIDE, 4, QB, 128), low(2 * SIDE, 4, QB, 128),
            low(SIDE, 2, 4, QB, 128), low(SIDE, 2, 4, QB, 128),
            low(*heads), low(*heads), low(*heads), low(*heads), low(SIDE, SIDE, QB, 128),
            low(GROUP, 512), low(SIDE, QB, 512),
            low(QB, 1024), low(QB, 3072), full(16, 2, 32, 256), low(16, 32, 256), low(16, 32, 256),
            low(SIDE, QB, 256), low(3, QB, 256), full(SIDE, 32, 256), full(3, 32, 256),
            full(SIDE, 8, 256), full(SIDE, 8, 256),
            dma(7), dma(3, 4), dma(3, 4), dma(2, 3), dma(2, 3), dma(3, 3), dma(3, 3),
            dma(4, 4), dma(4, 4), dma(4, 4), dma(4, 4),
            dma(3, 4), dma(3, 4), dma(3), dma(3), dma(2, 3), dma(2, 3),
            dma(4, 4), dma(4, 4), dma(4, 4), dma(4, 4), dma(10), dma(10),
        ],
        compiler_params=pltpu.CompilerParams(
            collective_id=0, has_side_effects=True, vmem_limit_bytes=VMEM_BYTES
        ),
        name="sublayer",
    )(nodes, w_qkv, w_out, grad_out, perm.reshape(1, GROUP), jnp.pad(blocks, ((0, 4), (0, 120))))
    return pl.pallas_call(
        hand_on, out_shape=shapes, in_specs=[vm] * 3, out_specs=(vm,) * 3, name="results"
    )(*results)


def solution(mesh):
    placed = (P(("seq", "blk"), None), P(), P(), P("seq"), P("seq", None), P(("seq", "blk"), None))
    return jax.shard_map(
        on_device,
        mesh=mesh,
        in_specs=placed,
        out_specs=(P(("seq", "blk"), None), P(("seq", "blk"), None), P(("seq", "blk"), None)),
        check_vma=False,
    )
```

```python
import jax
import jax.numpy as jnp
from jax import lax
from jax.experimental import pallas as pl
from jax.experimental.pallas import tpu as pltpu
from jax.sharding import PartitionSpec as P

HDIM = 64
QB = 128
GROUP = 512
SIDE = 4
BF = jnp.bfloat16
F32 = jnp.float32
MESH = pl.DeviceIdType.MESH
VMEM_BYTES = 56 * 1024 * 1024


def place():
    s = lax.axis_index("seq")
    z = lax.axis_index("blk")
    return s // 8, (s // 2) % 4, s % 2, z


def seq_of(x, y, c):
    return x * 8 + y * 2 + c


def turn(i, d):
    return lax.rem(i + (d + SIDE), SIDE)


def greet(x, y, c, z, y_steps):
    barrier = pltpu.get_barrier_semaphore()
    others = [(seq_of(x, y, c), turn(z, d)) for d in (1, 2, 3)]
    others += [(seq_of(turn(x, d), y, c), z) for d in (1, 2, 3)]
    others += [(seq_of(x, turn(y, d), c), z) for d in y_steps]
    others += [(seq_of(x, y, 1 - c), z)]
    for other in others:
        pl.semaphore_signal(barrier, inc=1, device_id=other, device_id_type=MESH)
    return lambda: pl.semaphore_wait(barrier, len(others))


def remote(src, dst, send_sem, recv_sem, device):
    return pltpu.make_async_remote_copy(
        src_ref=src,
        dst_ref=dst,
        send_sem=send_sem,
        recv_sem=recv_sem,
        device_id=device,
        device_id_type=MESH,
    )


def interleave(a, b):
    low = lax.broadcasted_iota(jnp.int32, a.shape, 1) < HDIM
    return (
        jnp.where(low, a, pltpu.roll(b, HDIM, 1)),
        jnp.where(low, pltpu.roll(a, HDIM, 1), b),
    )


def dot(a, b, ca=1, cb=0):
    return lax.dot_general(a, b, (((ca,), (cb,)), ((), ())), preferred_element_type=F32)


def store_pairs(ref, a, b):
    for half in range(2):
        cols = slice(128 * half, 128 * half + 128)
        first, second = interleave(a[:, cols], b[:, cols])
        ref[:, 256 * half : 256 * half + 128] = first.astype(BF)
        ref[:, 256 * half + 128 : 256 * half + 256] = second.astype(BF)


def plan_sums(blk_all, plan):
    shape = (QB, QB)
    lane = lax.broadcasted_iota(jnp.int32, (1, QB), 1)
    flat = jnp.zeros((1, QB), jnp.int32)
    for j in range(16):
        row = jnp.where(lane < 8, blk_all[j // 4, j % 4 : j % 4 + 1, :], 0)
        flat += pltpu.roll(row, 8 * j, 1) if j else row
    down = lax.broadcasted_iota(jnp.int32, shape, 0)
    across = lax.broadcasted_iota(jnp.int32, shape, 1)
    by_lane = jnp.broadcast_to(flat, shape)
    by_row = by_lane.T

    def total(values):
        return jnp.sum(values, axis=0, keepdims=True)

    def count(hits):
        return total(jnp.where(hits, 1, 0))

    rank = count((by_row < by_lane) | ((by_row == by_lane) & (down < across)))
    hits = jnp.broadcast_to(rank, shape).T == across
    order = total(jnp.where(hits, down, 0))
    sorted_ids = total(jnp.where(hits, by_row, 0))
    goes_on = jnp.where((sorted_ids == pltpu.roll(sorted_ids, 1, 1)) & (lane > 0), 1, 0)
    last = jnp.where(count(by_row == across) > 0, count(by_row <= across) - 1, QB)
    plan[...] = jnp.concatenate([order, goes_on, last, jnp.zeros((5, QB), jnp.int32)], axis=0)


def sublayer_kernel(
    nodes_in, w_qkv, w_out, go_in, perm, blk, out, grad_nodes, w_grad,
    nodes, go, wbuf, wobuf, pick, place_hits,
    zs_kv, zr_kv, zs_qg, zr_qg, xs_kv, xs_qg, kv_all, qg_all, blk_all, go_all,
    blk_pad, plan, plan_s, listed, keys, parts, seg, dqa,
    dkv, side, opp, y_recv, y_send, bxs_kv, bxr_kv, bxr_qa, bzs_kv, bzr_kv, bzs_qa, bzr_qa,
    mixed, gproj, gacc, wpart, wc_send, wc_recv, wx_send, wx_recv, wy_send, wy_recv, wz_send, wz_recv,
    w_sem, zk_s, zk_r, zs_sem, zr_sem, xs_sem, xr_sem, ys_sem, yr_sem, cs_sem, cr_sem,
    bzk_s, bzk_r, bzs_sem, bzr_sem, bxs_sem, bxr_sem, bys_sem, byr_sem, bcs_sem, bcr_sem, ws_sem, wr_sem,
):
    x, y, c, z = place()
    group = seq_of(x, y, c)
    sibling = (seq_of(x, y, 1 - c), z)
    order = (2, 1, 3, 0)
    kv_cols = pl.ds(1024, 2048)
    loads = [
        pltpu.make_async_copy(src, dst, w_sem.at[i])
        for i, (src, dst) in enumerate((
            (nodes_in, nodes),
            (w_qkv.at[:, kv_cols], wbuf.at[:, kv_cols]),
            (w_qkv.at[:, pl.ds(0, 1024)], wbuf.at[:, pl.ds(0, 1024)]),
            (go_in, go),
            (w_out, wobuf),
        ))
    ]
    for load in loads:
        load.start()
    ready = greet(x, y, c, z, (1, 2, 3))
    own_rows = pl.ds(pl.multiple_of(z * QB, QB), QB)

    def zk_copy(d, i):
        to, head = turn(z, d), turn(x, i)
        return remote(
            zs_kv.at[to, head], zr_kv.at[head, own_rows], zk_s.at[d - 1, i], zk_r.at[d - 1, i], (group, to)
        )

    def z_copy(which, d):
        to = turn(z, d)
        src = zs_qg.at[to] if which == 0 else go
        dst = (zr_qg, go_all)[which].at[own_rows]
        return remote(src, dst, zs_sem.at[which, d - 1], zr_sem.at[which, d - 1], (group, to))

    def project(first, second, put):
        for half in range(2):
            cols = slice(128 * half, 128 * half + 128)
            a, b = interleave(first[:, cols], second[:, cols])
            put(2 * half, a.astype(BF))
            put(2 * half + 1, b.astype(BF))

    def group_rows(g):
        return kv_all.at[pl.ds(pl.multiple_of(4 * g, 4), 4)]

    def x_copy(which, d):
        to = turn(x, d)
        src = (xs_kv, xs_qg)[which].at[to]
        dst = group_rows(group) if which == 0 else qg_all.at[x]
        return remote(src, dst, xs_sem.at[which, d - 1], xr_sem.at[which, d - 1], (seq_of(to, y, c), z))

    def y_copy(d, k):
        mine = group_rows(seq_of(turn(x, -d), y, c))
        to = seq_of(x, turn(y, (1, 3)[k]), c)
        return remote(mine, mine, ys_sem.at[d, k], yr_sem.at[d, k], (to, z))

    def relay(d, k):
        step = (1, 3)[k]
        first = pl.multiple_of(4 * seq_of(turn(x, -d), turn(y, -step), c) + 2 * k, 2)
        got = kv_all.at[pl.ds(first, 2)]
        return remote(got, got, ys_sem.at[d, 2 + k], yr_sem.at[d, 2 + k], (seq_of(x, turn(y, step), c), z))

    def cross(d, k):
        got = group_rows(seq_of(turn(x, -d), turn(y, -k), c))
        return remote(got, got, cs_sem.at[d, k], cr_sem.at[d, k], sibling)

    def pass_on(d):
        y_copy(d, 0).start()
        y_copy(d, 1).start()
        cross(d, 0).start()

    def relay_on(d):
        for k in range(2):
            y_copy(d, k).wait_recv()
            relay(d, k).start()
            cross(d, (1, 3)[k]).start()

    loads[0].wait()
    loads[1].wait()
    for d in (2, 1, 3, 0):
        to = turn(z, d)
        off = pl.multiple_of(to * 256, 256)
        k = dot(nodes[...], wbuf[:, pl.ds(1024 + off, 256)])
        v = dot(nodes[...], wbuf[:, pl.ds(2048 + off, 256)])
        if d == 2:
            ready()
        if d:
            def put(h, val):
                zs_kv[to, h] = val
            project(k, v, put)
            zk_copy(d, 0).start()
        else:
            def put(h, val):
                zr_kv[h, own_rows] = val
            project(k, v, put)
    for i in (1, 3, 2):
        for d in (2, 1, 3):
            zk_copy(d, i).start()

    local = perm[...] - group * GROUP
    hits = lax.broadcasted_iota(jnp.int32, (GROUP, GROUP), 0) == local
    one_hot = jnp.where(hits, 1.0, 0.0)
    pick[...] = one_hot.T.astype(BF)
    place_hits[...] = one_hot.astype(BF)

    blk_pad[...] = jnp.zeros_like(blk_pad)
    blk_pad[0:4, 0:8] = blk[...]
    blk_copies = [
        remote(blk_pad, blk_all.at[x], xs_sem.at[2, d - 1], xr_sem.at[2, d - 1], (seq_of(turn(x, d), y, c), z))
        for d in (1, 2, 3)
    ]
    for copy in blk_copies:
        copy.start()
    blk_all[x] = blk_pad[...]

    for load in loads[2:]:
        load.wait()
    for d in (2, 1, 3, 0):
        to = turn(z, d)
        off = pl.multiple_of(to * 256, 256)
        q = dot(nodes[...], wbuf[:, pl.ds(off, 256)])
        g = dot(go[...], wobuf[pl.ds(off, 256), :], 1, 1)
        if d:
            store_pairs(zs_qg.at[to], q, g)
        else:
            store_pairs(zr_qg.at[own_rows], q, g)
    go_all[own_rows] = go[...]

    for i in (0, 1, 3, 2):
        for d in (1, 2, 3):
            zk_copy(d, i).wait_recv()
        ordered = dot(pick[...], zr_kv[turn(x, i)]).astype(BF)
        if i:
            xs_kv[turn(x, i)] = ordered.reshape(4, QB, 128)
            x_copy(0, i).start()
        else:
            kv_all[pl.ds(pl.multiple_of(4 * group, 4), 4)] = ordered.reshape(4, QB, 128)
            pass_on(0)
            for d in (2, 1, 3):
                z_copy(0, d).start()

    relay_on(0)
    for d in (1, 3, 2):
        x_copy(0, d).wait_recv()
        pass_on(d)
    relay_on(1)
    for d in (1, 2, 3):
        z_copy(0, d).wait_recv()
    ordered = dot(pick[...], zr_qg[...])
    for h in range(SIDE):
        xs_qg[h] = ordered[:, 128 * h : 128 * h + 128].astype(BF)
    for d in (2, 1, 3):
        x_copy(1, d).start()
    for d in (2, 1, 3):
        z_copy(1, d).start()
    qg_all[x] = xs_qg[x]
    relay_on(3)

    for d in (1, 2, 3):
        blk_copies[d - 1].wait_recv()
    plan_sums(blk_all, plan)
    plan_copy = pltpu.make_async_copy(plan, plan_s, w_sem.at[5])
    listed_copy = pltpu.make_async_copy(blk_all, listed, w_sem.at[6])
    plan_copy.start()
    listed_copy.start()

    relay_on(2)
    for d in (0, 1, 3, 2):
        relay(d, 0).wait_recv()
        relay(d, 1).wait_recv()
        cross(d, 2).start()
    for d in (1, 2, 3):
        x_copy(1, d).wait_recv()
    plan_copy.wait()
    listed_copy.wait()
    for d in range(SIDE):
        for k in range(SIDE):
            cross(d, k).wait_recv()

    low = lax.broadcasted_iota(jnp.int32, (QB, QB), 1) < HDIM
    top = lax.broadcasted_iota(jnp.int32, (QB, QB), 0) < HDIM
    scale = HDIM ** (-0.5)

    def softmax_and_grad(i, u, kept):
        for t in range(8):
            kept[t * QB : (t + 1) * QB] = kv_all[listed[i, u, t]]
        qg = qg_all[i, u * QB : (u + 1) * QB].astype(F32)
        both = jnp.concatenate([jnp.where(low, qg * scale, 0.0), jnp.where(low, 0.0, qg)], axis=0).astype(BF)
        rows = dot(kept[...], both, 1, 1)
        scores, grad_scores = rows[:, :QB], rows[:, QB:]
        raised = jnp.exp(scores - jnp.max(scores, axis=0, keepdims=True))
        probs = raised * (1.0 / jnp.sum(raised, axis=0, keepdims=True))
        delta = jnp.sum(probs * grad_scores, axis=0, keepdims=True)
        grad_logits = (probs * (grad_scores - delta)).astype(BF)
        return both, jnp.concatenate([grad_logits, probs.astype(BF)], axis=1)

    def bx_qa(d):
        to = turn(x, d)
        return remote(
            dqa.at[to], bxr_qa.at[x], bxs_sem.at[1, d - 1], bxr_sem.at[1, d - 1], (seq_of(to, y, c), z)
        )

    def step(i, carry):
        pairs = [softmax_and_grad(i, u, keys.at[u]) for u in range(4)]
        for u, (both, pair) in enumerate(pairs):
            back = dot(keys[u], pair, 0, 0)
            dqa[i, u * QB : (u + 1) * QB] = jnp.where(top, back[:, :QB] * scale, back[:, QB:]).T.astype(BF)
            made = dot(pair, both).astype(BF)
            parts[pl.ds(pl.multiple_of(32 * i + 8 * u, 8), 8)] = made.reshape(8, QB, 128)
        return carry

    lax.fori_loop(0, 4, step, 0)
    for d in (2, 1, 3):
        bx_qa(d).start()
    bxr_qa[x] = dqa[x]

    def add_entry(i, run):
        run = run * plan_s[1, i].astype(F32) + parts[jnp.clip(plan_s[0, i], 0, QB - 1)].astype(F32)
        seg[i] = run
        return run

    seg[QB] = jnp.zeros((QB, 128), F32)
    lax.fori_loop(0, QB, add_entry, jnp.zeros((QB, 128), F32), unroll=4)

    def partial_sum(g, n):
        b = 4 * g + n
        return seg[jnp.clip(plan_s[2, b], 0, QB)]

    def bcross(d, k):
        return remote(dkv.at[d, k], side.at[d, k], bcs_sem.at[d, k], bcr_sem.at[d, k], sibling)

    def bx_kv(d):
        to = turn(x, d)
        return remote(
            bxs_kv.at[to], bxr_kv.at[x], bxs_sem.at[0, d - 1], bxr_sem.at[0, d - 1], (seq_of(to, y, c), z)
        )

    def bzk_copy(d, i):
        to, head = turn(z, d), turn(x, i)
        rows = pl.ds(pl.multiple_of(to * QB, QB), QB)
        return remote(bzs_kv.at[head, rows], bzr_kv.at[z, head], bzk_s.at[d - 1, i], bzk_r.at[d - 1, i], (group, to))

    def bzq_copy(d):
        to = turn(z, d)
        rows = pl.ds(pl.multiple_of(to * QB, QB), QB)
        return remote(bzs_qa.at[rows], bzr_qa.at[z], bzs_sem.at[d - 1], bzr_sem.at[d - 1], (group, to))

    def opposite(d, k):
        half = pl.ds(2 * k, 2)
        return remote(
            opp.at[d, half], opp.at[SIDE + d, half], bys_sem.at[d, k], byr_sem.at[d, k],
            (seq_of(x, turn(y, (1, 3)[k]), c), z),
        )

    def beside(d, k):
        return remote(
            y_send.at[d, k], y_recv.at[d, k], bys_sem.at[d, 2 + k], byr_sem.at[d, 2 + k],
            (seq_of(x, turn(y, (1, 3)[k]), c), z),
        )

    def paired(d, k, n):
        return partial_sum(seq_of(turn(x, d), turn(y, k), c), n) + side[d, k, n].astype(F32)

    def to_opposite(d):
        bcross(d, 2).wait_recv()
        for n in range(4):
            opp[d, n] = paired(d, 2, n).astype(BF)
        opposite(d, 0).start()
        opposite(d, 1).start()

    def to_neighbours(d):
        for k in range(2):
            bcross(d, (1, 3)[k]).wait_recv()
            opposite(d, k).wait_recv()
            for n in range(4):
                total = paired(d, (1, 3)[k], n)
                if n // 2 == k:
                    total += opp[SIDE + d, n].astype(F32)
                y_send[d, k, n] = total.astype(BF)
            beside(d, k).start()

    def settle(d):
        bcross(d, 0).wait_recv()
        for k in range(2):
            beside(d, k).wait_recv()
        for n in range(4):
            total = paired(d, 0, n) + (y_recv[d, 0, n].astype(F32) + y_recv[d, 1, n].astype(F32))
            rows = slice(QB * n, QB * n + QB)
            if d:
                bxs_kv[turn(x, d), rows] = total.astype(BF)
            else:
                bxr_kv[x, rows] = total.astype(BF)
        if d:
            bx_kv(d).start()

    def settle_z(i):
        head = turn(x, i)
        if i:
            bx_kv(SIDE - i).wait_recv()
        bzs_kv[head] = dot(place_hits[...], bxr_kv[head]).astype(BF)
        for d in (2, 1, 3):
            bzk_copy(d, i).start()
        bzr_kv[z, head] = bzs_kv[head, own_rows]

    def w_x(d):
        return remote(
            wx_send.at[turn(x, d)], wx_recv.at[d - 1],
            ws_sem.at[d], wr_sem.at[d], (seq_of(turn(x, d), y, c), z),
        )

    def w_y(d):
        return remote(
            wy_send.at[turn(y, d)], wy_recv.at[d - 1],
            ws_sem.at[3 + d], wr_sem.at[3 + d], (seq_of(x, turn(y, d), c), z),
        )

    def w_z(d):
        return remote(
            wz_send.at[turn(z, d)], wz_recv.at[z], ws_sem.at[6 + d], wr_sem.at[6 + d], (group, turn(z, d))
        )

    for k in (2, 1, 3, 0):
        for d in order:
            for n in range(4):
                dkv[d, k, n] = partial_sum(seq_of(turn(x, d), turn(y, k), 1 - c), n).astype(BF)
            bcross(d, k).start()
    for d in order:
        to_opposite(d)
    for d in order:
        to_neighbours(d)

    for d in (1, 2, 3):
        bx_qa(d).wait_recv()
    for h in range(SIDE):
        bzs_qa[:, 128 * h : 128 * h + 128] = dot(place_hits[...], bxr_qa[h]).astype(BF)
    for d in (2, 1, 3):
        bzq_copy(d).start()
    bzr_qa[z] = bzs_qa[own_rows]

    for d in (1, 2, 3):
        z_copy(1, d).wait_recv()
    group_mixed = []
    for half in range(2):
        a = bzs_qa[:, 256 * half : 256 * half + 128].astype(F32)
        b = bzs_qa[:, 256 * half + 128 : 256 * half + 256].astype(F32)
        group_mixed.append(interleave(a, b)[1].astype(BF))
    group_mixed = jnp.concatenate(group_mixed, axis=1)
    for i in range(SIDE):
        part = dot(go_all[:, 256 * i : 256 * i + 256], group_mixed, 0, 0)
        wpart[4 * i : 4 * i + 4] = part.reshape(4, 2, 32, 256)
    w_cross = remote(wc_send, wc_recv, ws_sem.at[0], wr_sem.at[0], sibling)
    wc_send[...] = wpart[:, 1 - c].astype(BF)
    w_cross.start()

    for d in (1, 2, 3):
        x_copy(0, d).wait_send()
        x_copy(1, d).wait_send()
        z_copy(0, d).wait_send()
        z_copy(1, d).wait_send()
        bx_qa(d).wait_send()
        blk_copies[d - 1].wait_send()
        for i in range(SIDE):
            zk_copy(d, i).wait_send()
    for d in range(SIDE):
        for k in range(2):
            y_copy(d, k).wait_send()
            relay(d, k).wait_send()
            opposite(d, k).wait_send()
        for k in range(SIDE):
            cross(d, k).wait_send()
            bcross(d, k).wait_send()

    settle(2)
    settle(1)
    w_cross.wait_recv()
    wsum = (wpart[:, c] + wc_recv[...].astype(F32)).reshape(SIDE, QB, 256)
    wx_send[...] = wsum.astype(BF)
    for d in (2, 1, 3):
        w_x(d).start()
    settle(3)
    settle_z(2)
    settle(0)
    settle_z(0)
    settle_z(3)
    settle_z(1)

    wrows = wx_send[x].astype(F32)
    for d in (1, 2, 3):
        w_x(d).wait_recv()
        wrows += wx_recv[d - 1].astype(F32)
    wy_send[...] = wrows.reshape(SIDE, 32, 256)
    for d in (2, 1, 3):
        w_y(d).start()

    for d in (1, 2, 3):
        bzq_copy(d).wait_recv()
    for h in range(SIDE):
        for half in range(2):
            a = bzr_qa[h, :, 256 * half : 256 * half + 128].astype(F32)
            b = bzr_qa[h, :, 256 * half + 128 : 256 * half + 256].astype(F32)
            cols = slice(256 * h + 128 * half, 256 * h + 128 * half + 128)
            first, second = interleave(a, b)
            gproj[:, cols] = first.astype(BF)
            mixed[:, cols] = second.astype(BF)
    out[...] = dot(mixed[...], wobuf[...]).astype(BF)
    for i in range(SIDE):
        rows = slice(256 * i, 256 * i + 256)
        gacc[:, rows] = dot(gproj[:, :1024], wbuf[rows, :1024], 1, 1)

    wrows = wy_send[y]
    for d in (1, 2, 3):
        w_y(d).wait_recv()
        wrows += wy_recv[d - 1]
    wz_send[...] = wrows.reshape(SIDE, 8, 256)
    for d in (2, 1, 3):
        w_z(d).start()
    wz_recv[z] = wz_send[z]

    for i in range(SIDE):
        for d in (1, 2, 3):
            bzk_copy(d, i).wait_recv()
    for h in range(SIDE):
        for half in range(2):
            a = bzr_kv[h, 2 * half].astype(F32)
            b = bzr_kv[h, 2 * half + 1].astype(F32)
            col = 256 * h + 128 * half
            first, second = interleave(a, b)
            gproj[:, 1024 + col : 1024 + col + 128] = first.astype(BF)
            gproj[:, 2048 + col : 2048 + col + 128] = second.astype(BF)
    for i in range(SIDE):
        rows = slice(256 * i, 256 * i + 256)
        grad_nodes[:, rows] = (gacc[:, rows] + dot(gproj[:, 1024:], wbuf[rows, 1024:], 1, 1)).astype(BF)

    for d in (1, 2, 3):
        w_z(d).wait_recv()
    for h in range(SIDE):
        w_grad[:, 256 * h : 256 * h + 256] = wz_recv[h]

    w_cross.wait_send()
    for d in (1, 2, 3):
        bx_kv(d).wait_send()
        bzq_copy(d).wait_send()
        w_z(d).wait_send()
        w_x(d).wait_send()
        w_y(d).wait_send()
        for i in range(SIDE):
            bzk_copy(d, i).wait_send()
    for d in range(SIDE):
        for k in range(2):
            beside(d, k).wait_send()


def hand_on(*refs):
    half = len(refs) // 2
    for i in range(half):
        refs[half + i][...] = refs[i][...]


def dma(*shape):
    return pltpu.SemaphoreType.DMA(shape)


def low_precision(*shape):
    return pltpu.VMEM(shape, BF)


def full(*shape):
    return pltpu.VMEM(shape, F32)


def on_device(nodes, w_qkv, w_out, perm, blocks, grad_out):
    vm = pl.BlockSpec(memory_space=pltpu.VMEM)
    anywhere = pl.BlockSpec(memory_space=pl.ANY)
    sds = jax.ShapeDtypeStruct
    shapes = (sds((QB, 1024), BF), sds((QB, 1024), BF), sds((8, 1024), F32))
    low = low_precision
    heads = (SIDE, GROUP, 128)
    results = pl.pallas_call(
        sublayer_kernel,
        out_shape=shapes,
        in_specs=[anywhere, anywhere, anywhere, anywhere, vm, vm],
        out_specs=(vm, vm, vm),
        scratch_shapes=[
            low(QB, 1024), low(QB, 1024), low(1024, 3072), low(1024, 1024), low(GROUP, GROUP), low(GROUP, GROUP),
            low(SIDE, SIDE, QB, 128), low(*heads), low(SIDE, QB, 512), low(GROUP, 512),
            low(SIDE, 4, QB, 128), low(*heads), low(QB, QB, 128), low(*heads),
            pltpu.VMEM((SIDE, 8, 128), jnp.int32), low(GROUP, 1024),
            pltpu.VMEM((8, QB), jnp.int32), pltpu.VMEM((8, QB), jnp.int32), pltpu.SMEM((8, QB), jnp.int32), pltpu.SMEM((SIDE, 8, 128), jnp.int32),
            low(4, 1024, 128), low(QB, QB, 128), full(QB + 1, QB, 128), low(*heads),
            low(SIDE, SIDE, 4, QB, 128), low(SIDE, SIDE, 4, QB, 128), low(2 * SIDE, 4, QB, 128),
            low(SIDE, 2, 4, QB, 128), low(SIDE, 2, 4, QB, 128),
            low(*heads), low(*heads), low(*heads), low(*heads), low(SIDE, SIDE, QB, 128),
            low(GROUP, 512), low(SIDE, QB, 512),
            low(QB, 1024), low(QB, 3072), full(QB, 1024), full(16, 2, 32, 256), low(16, 32, 256), low(16, 32, 256),
            low(SIDE, QB, 256), low(3, QB, 256), full(SIDE, 32, 256), full(3, 32, 256),
            full(SIDE, 8, 256), full(SIDE, 8, 256),
            dma(7), dma(3, 4), dma(3, 4), dma(2, 3), dma(2, 3), dma(3, 3), dma(3, 3),
            dma(4, 4), dma(4, 4), dma(4, 4), dma(4, 4),
            dma(3, 4), dma(3, 4), dma(3), dma(3), dma(2, 3), dma(2, 3),
            dma(4, 4), dma(4, 4), dma(4, 4), dma(4, 4), dma(10), dma(10),
        ],
        compiler_params=pltpu.CompilerParams(
            collective_id=0, has_side_effects=True, vmem_limit_bytes=VMEM_BYTES
        ),
        name="sublayer",
    )(nodes, w_qkv, w_out, grad_out, perm.reshape(1, GROUP), blocks)
    return pl.pallas_call(
        hand_on, out_shape=shapes, in_specs=[vm] * 3, out_specs=(vm,) * 3, name="results"
    )(*results)


def solution(mesh):
    placed = (P(("seq", "blk"), None), P(), P(), P("seq"), P("seq", None), P(("seq", "blk"), None))
    return jax.shard_map(
        on_device,
        mesh=mesh,
        in_specs=placed,
        out_specs=(P(("seq", "blk"), None), P(("seq", "blk"), None), P(("seq", "blk"), None)),
        check_vma=False,
    )
```

```python
import jax
import jax.numpy as jnp
from jax import lax
from jax.experimental import pallas as pl
from jax.experimental.pallas import tpu as pltpu
from jax.sharding import PartitionSpec as P

HDIM = 64
QB = 128
GROUP = 512
SIDE = 4
BF = jnp.bfloat16
F32 = jnp.float32
MESH = pl.DeviceIdType.MESH
VMEM_BYTES = 56 * 1024 * 1024


def place():
    s = lax.axis_index("seq")
    z = lax.axis_index("blk")
    return s // 8, (s // 2) % 4, s % 2, z


def seq_of(x, y, c):
    return x * 8 + y * 2 + c


def turn(i, d):
    return lax.rem(i + (d + SIDE), SIDE)


def greet(x, y, c, z, y_steps):
    barrier = pltpu.get_barrier_semaphore()
    others = [(seq_of(x, y, c), turn(z, d)) for d in (1, 2, 3)]
    others += [(seq_of(turn(x, d), y, c), z) for d in (1, 2, 3)]
    others += [(seq_of(x, turn(y, d), c), z) for d in y_steps]
    others += [(seq_of(x, y, 1 - c), z)]
    for other in others:
        pl.semaphore_signal(barrier, inc=1, device_id=other, device_id_type=MESH)
    return lambda: pl.semaphore_wait(barrier, len(others))


def remote(src, dst, send_sem, recv_sem, device):
    return pltpu.make_async_remote_copy(
        src_ref=src,
        dst_ref=dst,
        send_sem=send_sem,
        recv_sem=recv_sem,
        device_id=device,
        device_id_type=MESH,
    )


def interleave(a, b):
    low = lax.broadcasted_iota(jnp.int32, a.shape, 1) < HDIM
    return (
        jnp.where(low, a, pltpu.roll(b, HDIM, 1)),
        jnp.where(low, pltpu.roll(a, HDIM, 1), b),
    )


def dot(a, b, ca=1, cb=0):
    return lax.dot_general(a, b, (((ca,), (cb,)), ((), ())), preferred_element_type=F32)


def store_pairs(ref, a, b):
    for half in range(2):
        cols = slice(128 * half, 128 * half + 128)
        first, second = interleave(a[:, cols], b[:, cols])
        ref[:, 256 * half : 256 * half + 128] = first.astype(BF)
        ref[:, 256 * half + 128 : 256 * half + 256] = second.astype(BF)


def plan_sums(blk_all, plan):
    shape = (QB, QB)
    lane = lax.broadcasted_iota(jnp.int32, (1, QB), 1)
    flat = jnp.zeros((1, QB), jnp.int32)
    for j in range(16):
        row = jnp.where(lane < 8, blk_all[j // 4, j % 4 : j % 4 + 1, :], 0)
        flat += pltpu.roll(row, 8 * j, 1) if j else row
    down = lax.broadcasted_iota(jnp.int32, shape, 0)
    across = lax.broadcasted_iota(jnp.int32, shape, 1)
    by_lane = jnp.broadcast_to(flat, shape)
    by_row = by_lane.T

    def total(values):
        return jnp.sum(values, axis=0, keepdims=True)

    def count(hits):
        return total(jnp.where(hits, 1, 0))

    rank = count((by_row < by_lane) | ((by_row == by_lane) & (down < across)))
    hits = jnp.broadcast_to(rank, shape).T == across
    order = total(jnp.where(hits, down, 0))
    sorted_ids = total(jnp.where(hits, by_row, 0))
    goes_on = jnp.where((sorted_ids == pltpu.roll(sorted_ids, 1, 1)) & (lane > 0), 1, 0)
    last = jnp.where(count(by_row == across) > 0, count(by_row <= across) - 1, QB)
    plan[...] = jnp.concatenate([order, goes_on, last, jnp.zeros((5, QB), jnp.int32)], axis=0)


def sublayer_kernel(
    nodes_in, w_qkv, w_out, go_in, perm, blk, out, grad_nodes, w_grad,
    nodes, go, wbuf, wobuf, pick, place_hits,
    zs_kv, zr_kv, zs_qg, zr_qg, xs_kv, xs_qg, kv_all, qg_all, blk_all, go_all,
    blk_pad, plan, plan_s, listed, keys, parts, seg, dqa,
    dkv, side, opp, y_recv, y_send, bxs_kv, bxr_kv, bxr_qa, bzs_kv, bzr_kv, bzs_qa, bzr_qa,
    mixed, gproj, gacc, wpart, wc_send, wc_recv, wx_send, wx_recv, wy_send, wy_recv, wz_send, wz_recv,
    w_sem, send, zk_r, zr_sem, xr_sem, yr_sem, rr_sem, cr_sem,
    bzr_sem, bxr_sem, byr_sem, bcr_sem, wr_sem,
):
    x, y, c, z = place()
    group = seq_of(x, y, c)
    sibling = (seq_of(x, y, 1 - c), z)
    order = (2, 1, 3, 0)
    kv_cols = pl.ds(1024, 2048)
    loads = [
        pltpu.make_async_copy(src, dst, w_sem.at[i])
        for i, (src, dst) in enumerate((
            (nodes_in, nodes),
            (w_qkv.at[:, kv_cols], wbuf.at[:, kv_cols]),
            (w_qkv.at[:, pl.ds(0, 1024)], wbuf.at[:, pl.ds(0, 1024)]),
            (go_in, go),
            (w_out, wobuf),
        ))
    ]
    for load in loads:
        load.start()
    ready = greet(x, y, c, z, (1, 2, 3))
    own_rows = pl.ds(pl.multiple_of(z * QB, QB), QB)

    def arrived(ref, sem):
        remote(ref, ref, send.at[0], sem, sibling).wait_recv()

    def sent(blocks, i):
        ref = kv_all.at[pl.ds(0, blocks)]
        remote(ref, ref, send.at[i], cr_sem.at[0], sibling).wait_send()

    def zk_copy(d, i):
        to, head = turn(z, d), turn(x, i)
        return remote(
            zs_kv.at[to, head], zr_kv.at[head, own_rows], send.at[0], zk_r.at[i], (group, to)
        )

    def z_copy(which, d):
        to = turn(z, d)
        src = zs_qg.at[to] if which == 0 else go
        dst = (zr_qg, go_all)[which].at[own_rows]
        return remote(src, dst, send.at[0], zr_sem.at[which], (group, to))

    def project(first, second, put):
        for half in range(2):
            cols = slice(128 * half, 128 * half + 128)
            a, b = interleave(first[:, cols], second[:, cols])
            put(2 * half, a.astype(BF))
            put(2 * half + 1, b.astype(BF))

    def group_rows(g):
        return kv_all.at[pl.ds(pl.multiple_of(4 * g, 4), 4)]

    def x_copy(which, d):
        to = turn(x, d)
        src = (xs_kv, xs_qg)[which].at[to]
        dst = group_rows(group) if which == 0 else qg_all.at[x]
        sem = xr_sem.at[d - 1] if which == 0 else xr_sem.at[3]
        return remote(src, dst, send.at[1 - which], sem, (seq_of(to, y, c), z))

    def y_copy(d, k, h):
        half = k if h == 0 else 1 - k
        first = pl.multiple_of(4 * seq_of(turn(x, -d), y, c) + 2 * half, 2)
        mine = kv_all.at[pl.ds(first, 2)]
        to = seq_of(x, turn(y, (1, 3)[k]), c)
        return remote(mine, mine, send.at[1], yr_sem.at[d, k, h], (to, z))

    def relay(d, k):
        step = (1, 3)[k]
        first = pl.multiple_of(4 * seq_of(turn(x, -d), turn(y, -step), c) + 2 * k, 2)
        got = kv_all.at[pl.ds(first, 2)]
        return remote(got, got, send.at[1], rr_sem.at[d], (seq_of(x, turn(y, step), c), z))

    def cross(d, k):
        got = group_rows(seq_of(turn(x, -d), turn(y, -k), c))
        return remote(got, got, send.at[1], cr_sem.at[0], sibling)

    def pass_on(d):
        for h in range(2):
            for k in range(2):
                y_copy(d, k, h).start()
        cross(d, 0).start()

    def relay_on(d):
        for k in range(2):
            y_copy(d, k, 0).wait_recv()
            relay(d, k).start()
        for k in range(2):
            y_copy(d, k, 1).wait_recv()
            cross(d, (1, 3)[k]).start()

    loads[0].wait()
    loads[1].wait()
    for d in (2, 1, 3, 0):
        to = turn(z, d)
        off = pl.multiple_of(to * 256, 256)
        k = dot(nodes[...], wbuf[:, pl.ds(1024 + off, 256)])
        v = dot(nodes[...], wbuf[:, pl.ds(2048 + off, 256)])
        if d == 2:
            ready()
        if d:
            def put(h, val):
                zs_kv[to, h] = val
            project(k, v, put)
            zk_copy(d, 0).start()
        else:
            def put(h, val):
                zr_kv[h, own_rows] = val
            project(k, v, put)
    for i in (1, 3, 2):
        for d in (2, 1, 3):
            zk_copy(d, i).start()

    local = perm[...] - group * GROUP
    hits = lax.broadcasted_iota(jnp.int32, (GROUP, GROUP), 0) == local
    one_hot = jnp.where(hits, 1.0, 0.0)
    pick[...] = one_hot.T.astype(BF)
    place_hits[...] = one_hot.astype(BF)

    blk_pad[...] = jnp.zeros_like(blk_pad)
    blk_pad[0:4, 0:8] = blk[...]
    blk_copies = [
        remote(blk_pad, blk_all.at[x], send.at[2], xr_sem.at[4], (seq_of(turn(x, d), y, c), z))
        for d in (1, 2, 3)
    ]
    for copy in blk_copies:
        copy.start()
    blk_all[x] = blk_pad[...]

    for load in loads[2:]:
        load.wait()
    for d in (2, 1, 3, 0):
        to = turn(z, d)
        off = pl.multiple_of(to * 256, 256)
        q = dot(nodes[...], wbuf[:, pl.ds(off, 256)])
        g = dot(go[...], wobuf[pl.ds(off, 256), :], 1, 1)
        if d:
            store_pairs(zs_qg.at[to], q, g)
        else:
            store_pairs(zr_qg.at[own_rows], q, g)
    go_all[own_rows] = go[...]

    for i in (0, 1, 3, 2):
        arrived(zr_kv.at[0, pl.ds(0, 3 * QB)], zk_r.at[i])
        ordered = dot(pick[...], zr_kv[turn(x, i)]).astype(BF)
        if i:
            xs_kv[turn(x, i)] = ordered.reshape(4, QB, 128)
            x_copy(0, i).start()
        else:
            kv_all[pl.ds(pl.multiple_of(4 * group, 4), 4)] = ordered.reshape(4, QB, 128)
            pass_on(0)
            for d in (2, 1, 3):
                z_copy(0, d).start()

    relay_on(0)
    for d in (1, 3, 2):
        x_copy(0, d).wait_recv()
        pass_on(d)
    relay_on(1)
    arrived(zr_qg.at[pl.ds(0, 3 * QB)], zr_sem.at[0])
    ordered = dot(pick[...], zr_qg[...])
    for h in range(SIDE):
        xs_qg[h] = ordered[:, 128 * h : 128 * h + 128].astype(BF)
    for d in (2, 1, 3):
        x_copy(1, d).start()
    for d in (2, 1, 3):
        z_copy(1, d).start()
    qg_all[x] = xs_qg[x]
    relay_on(3)

    arrived(blk_all.at[pl.ds(0, 3)], xr_sem.at[4])
    plan_sums(blk_all, plan)
    plan_copy = pltpu.make_async_copy(plan, plan_s, w_sem.at[5])
    listed_copy = pltpu.make_async_copy(blk_all, listed, w_sem.at[6])
    plan_copy.start()
    listed_copy.start()

    relay_on(2)
    for d in (0, 1, 3, 2):
        arrived(group_rows(seq_of(turn(x, -d), turn(y, 2), c)), rr_sem.at[d])
        cross(d, 2).start()
    arrived(qg_all.at[pl.ds(0, 3)], xr_sem.at[3])
    plan_copy.wait()
    listed_copy.wait()
    arrived(kv_all.at[pl.ds(0, 64)], cr_sem.at[0])

    low = lax.broadcasted_iota(jnp.int32, (QB, QB), 1) < HDIM
    top = lax.broadcasted_iota(jnp.int32, (QB, QB), 0) < HDIM
    scale = HDIM ** (-0.5)

    def softmax_and_grad(i, u, kept):
        for t in range(8):
            kept[t * QB : (t + 1) * QB] = kv_all[listed[i, u, t]]
        qg = qg_all[i, u * QB : (u + 1) * QB].astype(F32)
        both = jnp.concatenate([jnp.where(low, qg * scale, 0.0), jnp.where(low, 0.0, qg)], axis=0).astype(BF)
        rows = dot(kept[...], both, 1, 1)
        scores, grad_scores = rows[:, :QB], rows[:, QB:]
        raised = jnp.exp(scores - jnp.max(scores, axis=0, keepdims=True))
        probs = raised * (1.0 / jnp.sum(raised, axis=0, keepdims=True))
        delta = jnp.sum(probs * grad_scores, axis=0, keepdims=True)
        grad_logits = (probs * (grad_scores - delta)).astype(BF)
        return both, jnp.concatenate([grad_logits, probs.astype(BF)], axis=1)

    def bx_qa(d):
        to = turn(x, d)
        return remote(
            dqa.at[to], bxr_qa.at[x], send.at[4], bxr_sem.at[3], (seq_of(to, y, c), z)
        )

    def step(i, carry):
        pairs = [softmax_and_grad(i, u, keys.at[u]) for u in range(4)]
        for u, (both, pair) in enumerate(pairs):
            back = dot(keys[u], pair, 0, 0)
            dqa[i, u * QB : (u + 1) * QB] = jnp.where(top, back[:, :QB] * scale, back[:, QB:]).T.astype(BF)
            made = dot(pair, both).astype(BF)
            parts[pl.ds(pl.multiple_of(32 * i + 8 * u, 8), 8)] = made.reshape(8, QB, 128)
        return carry

    lax.fori_loop(0, 4, step, 0)
    for d in (2, 1, 3):
        bx_qa(d).start()
    bxr_qa[x] = dqa[x]

    def add_entry(i, run):
        run = run * plan_s[1, i].astype(F32) + parts[jnp.clip(plan_s[0, i], 0, QB - 1)].astype(F32)
        seg[i] = run
        return run

    seg[QB] = jnp.zeros((QB, 128), F32)
    lax.fori_loop(0, QB, add_entry, jnp.zeros((QB, 128), F32), unroll=4)

    def partial_sum(g, n):
        b = 4 * g + n
        return seg[jnp.clip(plan_s[2, b], 0, QB)]

    def bcross(d, k):
        return remote(dkv.at[k, d], side.at[k, d], send.at[3], bcr_sem.at[k], sibling)

    def bx_kv(d):
        to = turn(x, d)
        return remote(
            bxs_kv.at[to], bxr_kv.at[x], send.at[3], bxr_sem.at[d - 1], (seq_of(to, y, c), z)
        )

    def bzk_copy(d, i):
        to, head = turn(z, d), turn(x, i)
        rows = pl.ds(pl.multiple_of(to * QB, QB), QB)
        return remote(bzs_kv.at[head, rows], bzr_kv.at[z, head], send.at[4], bzr_sem.at[0], (group, to))

    def bzq_copy(d):
        to = turn(z, d)
        rows = pl.ds(pl.multiple_of(to * QB, QB), QB)
        return remote(bzs_qa.at[rows], bzr_qa.at[z], send.at[4], bzr_sem.at[1], (group, to))

    def opposite(d, k):
        half = pl.ds(2 * k, 2)
        return remote(
            opp.at[d, half], opp.at[SIDE + d, half], send.at[3], byr_sem.at[d],
            (seq_of(x, turn(y, (1, 3)[k]), c), z),
        )

    def beside(d, k):
        return remote(
            y_send.at[d, k], y_recv.at[d, k], send.at[3], byr_sem.at[SIDE + d],
            (seq_of(x, turn(y, (1, 3)[k]), c), z),
        )

    def paired(d, k, n):
        return partial_sum(seq_of(turn(x, d), turn(y, k), c), n) + side[k, d, n].astype(F32)

    def to_opposite(d):
        for n in range(4):
            opp[d, n] = paired(d, 2, n).astype(BF)
        opposite(d, 0).start()
        opposite(d, 1).start()

    def to_neighbours(d):
        arrived(opp.at[SIDE + d], byr_sem.at[d])
        for k in range(2):
            for n in range(4):
                total = paired(d, (1, 3)[k], n)
                if n // 2 == k:
                    total += opp[SIDE + d, n].astype(F32)
                y_send[d, k, n] = total.astype(BF)
            beside(d, k).start()

    def settle(d):
        arrived(y_recv.at[d], byr_sem.at[SIDE + d])
        for n in range(4):
            total = paired(d, 0, n) + (y_recv[d, 0, n].astype(F32) + y_recv[d, 1, n].astype(F32))
            rows = slice(QB * n, QB * n + QB)
            if d:
                bxs_kv[turn(x, d), rows] = total.astype(BF)
            else:
                bxr_kv[x, rows] = total.astype(BF)
        if d:
            bx_kv(d).start()

    def settle_z(i):
        head = turn(x, i)
        if i:
            bx_kv(SIDE - i).wait_recv()
        bzs_kv[head] = dot(place_hits[...], bxr_kv[head]).astype(BF)
        for d in (2, 1, 3):
            bzk_copy(d, i).start()
        bzr_kv[z, head] = bzs_kv[head, own_rows]

    def w_x(d):
        return remote(
            wx_send.at[turn(x, d)], wx_recv.at[d - 1],
            send.at[4], wr_sem.at[1], (seq_of(turn(x, d), y, c), z),
        )

    def w_y(d):
        return remote(
            wy_send.at[turn(y, d)], wy_recv.at[d - 1],
            send.at[4], wr_sem.at[2], (seq_of(x, turn(y, d), c), z),
        )

    def w_z(d):
        return remote(
            wz_send.at[turn(z, d)], wz_recv.at[z], send.at[5], wr_sem.at[3], (group, turn(z, d))
        )

    for k in (2, 1, 3, 0):
        for d in order:
            for n in range(4):
                dkv[k, d, n] = partial_sum(seq_of(turn(x, d), turn(y, k), 1 - c), n).astype(BF)
            bcross(d, k).start()
    arrived(side.at[2], bcr_sem.at[2])
    for d in order:
        to_opposite(d)
    arrived(side.at[1], bcr_sem.at[1])
    arrived(side.at[3], bcr_sem.at[3])
    for d in order:
        to_neighbours(d)

    arrived(bxr_qa.at[pl.ds(0, 3)], bxr_sem.at[3])
    for h in range(SIDE):
        bzs_qa[:, 128 * h : 128 * h + 128] = dot(place_hits[...], bxr_qa[h]).astype(BF)
    for d in (2, 1, 3):
        bzq_copy(d).start()
    bzr_qa[z] = bzs_qa[own_rows]

    arrived(go_all.at[pl.ds(0, 3 * QB)], zr_sem.at[1])
    group_mixed = []
    for half in range(2):
        a = bzs_qa[:, 256 * half : 256 * half + 128].astype(F32)
        b = bzs_qa[:, 256 * half + 128 : 256 * half + 256].astype(F32)
        group_mixed.append(interleave(a, b)[1].astype(BF))
    group_mixed = jnp.concatenate(group_mixed, axis=1)
    for i in range(SIDE):
        part = dot(go_all[:, 256 * i : 256 * i + 256], group_mixed, 0, 0)
        wpart[4 * i : 4 * i + 4] = part.reshape(4, 2, 32, 256)
    w_cross = remote(wc_send, wc_recv, send.at[4], wr_sem.at[0], sibling)
    wc_send[...] = wpart[:, 1 - c].astype(BF)
    w_cross.start()

    sent(60, 0)
    sent(124, 1)
    blocks_sent = blk_all.at[pl.ds(0, 3)]
    remote(blocks_sent, blocks_sent, send.at[2], xr_sem.at[4], sibling).wait_send()
    arrived(side.at[0], bcr_sem.at[0])

    settle(2)
    settle(1)
    w_cross.wait_recv()
    wsum = (wpart[:, c] + wc_recv[...].astype(F32)).reshape(SIDE, QB, 256)
    wx_send[...] = wsum.astype(BF)
    for d in (2, 1, 3):
        w_x(d).start()
    settle(3)
    settle_z(2)
    settle(0)
    settle_z(0)
    settle_z(3)
    settle_z(1)

    wrows = wx_send[x].astype(F32)
    arrived(wx_recv, wr_sem.at[1])
    for d in (1, 2, 3):
        wrows += wx_recv[d - 1].astype(F32)
    wy_send[...] = wrows.reshape(SIDE, 32, 256)
    for d in (2, 1, 3):
        w_y(d).start()

    arrived(bzr_qa.at[pl.ds(0, 3)], bzr_sem.at[1])
    for h in range(SIDE):
        for half in range(2):
            a = bzr_qa[h, :, 256 * half : 256 * half + 128].astype(F32)
            b = bzr_qa[h, :, 256 * half + 128 : 256 * half + 256].astype(F32)
            cols = slice(256 * h + 128 * half, 256 * h + 128 * half + 128)
            first, second = interleave(a, b)
            gproj[:, cols] = first.astype(BF)
            mixed[:, cols] = second.astype(BF)
    out[...] = dot(mixed[...], wobuf[...]).astype(BF)
    for i in range(SIDE):
        rows = slice(256 * i, 256 * i + 256)
        gacc[:, rows] = dot(gproj[:, :1024], wbuf[rows, :1024], 1, 1)

    wrows = wy_send[y]
    arrived(wy_recv, wr_sem.at[2])
    for d in (1, 2, 3):
        wrows += wy_recv[d - 1]
    wz_send[...] = wrows.reshape(SIDE, 8, 256)
    for d in (2, 1, 3):
        w_z(d).start()
    wz_recv[z] = wz_send[z]

    arrived(bzr_kv.at[pl.ds(0, 3)], bzr_sem.at[0])
    for h in range(SIDE):
        for half in range(2):
            a = bzr_kv[h, 2 * half].astype(F32)
            b = bzr_kv[h, 2 * half + 1].astype(F32)
            col = 256 * h + 128 * half
            first, second = interleave(a, b)
            gproj[:, 1024 + col : 1024 + col + 128] = first.astype(BF)
            gproj[:, 2048 + col : 2048 + col + 128] = second.astype(BF)
    for i in range(SIDE):
        rows = slice(256 * i, 256 * i + 256)
        grad_nodes[:, rows] = (gacc[:, rows] + dot(gproj[:, 1024:], wbuf[rows, 1024:], 1, 1)).astype(BF)

    arrived(wz_recv.at[pl.ds(0, 3)], wr_sem.at[3])
    for h in range(SIDE):
        w_grad[:, 256 * h : 256 * h + 256] = wz_recv[h]

    sent(124, 3)
    sent(53, 4)
    third = wz_send.at[pl.ds(0, 3)]
    remote(third, third, send.at[5], wr_sem.at[3], sibling).wait_send()


def hand_on(*refs):
    half = len(refs) // 2
    for i in range(half):
        refs[half + i][...] = refs[i][...]


def dma(*shape):
    return pltpu.SemaphoreType.DMA(shape)


def low_precision(*shape):
    return pltpu.VMEM(shape, BF)


def full(*shape):
    return pltpu.VMEM(shape, F32)


def on_device(nodes, w_qkv, w_out, perm, blocks, grad_out):
    vm = pl.BlockSpec(memory_space=pltpu.VMEM)
    anywhere = pl.BlockSpec(memory_space=pl.ANY)
    sds = jax.ShapeDtypeStruct
    shapes = (sds((QB, 1024), BF), sds((QB, 1024), BF), sds((8, 1024), F32))
    low = low_precision
    heads = (SIDE, GROUP, 128)
    results = pl.pallas_call(
        sublayer_kernel,
        out_shape=shapes,
        in_specs=[anywhere, anywhere, anywhere, anywhere, vm, vm],
        out_specs=(vm, vm, vm),
        scratch_shapes=[
            low(QB, 1024), low(QB, 1024), low(1024, 3072), low(1024, 1024), low(GROUP, GROUP), low(GROUP, GROUP),
            low(SIDE, SIDE, QB, 128), low(*heads), low(SIDE, QB, 512), low(GROUP, 512),
            low(SIDE, 4, QB, 128), low(*heads), low(QB, QB, 128), low(*heads),
            pltpu.VMEM((SIDE, 8, 128), jnp.int32), low(GROUP, 1024),
            pltpu.VMEM((8, QB), jnp.int32), pltpu.VMEM((8, QB), jnp.int32), pltpu.SMEM((8, QB), jnp.int32), pltpu.SMEM((SIDE, 8, 128), jnp.int32),
            low(4, 1024, 128), low(QB, QB, 128), full(QB + 1, QB, 128), low(*heads),
            low(SIDE, SIDE, 4, QB, 128), low(SIDE, SIDE, 4, QB, 128), low(2 * SIDE, 4, QB, 128),
            low(SIDE, 2, 4, QB, 128), low(SIDE, 2, 4, QB, 128),
            low(*heads), low(*heads), low(*heads), low(*heads), low(SIDE, SIDE, QB, 128),
            low(GROUP, 512), low(SIDE, QB, 512),
            low(QB, 1024), low(QB, 3072), full(QB, 1024), full(16, 2, 32, 256), low(16, 32, 256), low(16, 32, 256),
            low(SIDE, QB, 256), low(3, QB, 256), full(SIDE, 32, 256), full(3, 32, 256),
            full(SIDE, 8, 256), full(SIDE, 8, 256),
            dma(7), dma(6), dma(4), dma(2), dma(5), dma(4, 2, 2), dma(4), dma(1),
            dma(2), dma(4), dma(8), dma(4), dma(4),
        ],
        compiler_params=pltpu.CompilerParams(
            collective_id=0, has_side_effects=True, vmem_limit_bytes=VMEM_BYTES
        ),
        name="sublayer",
    )(nodes, w_qkv, w_out, grad_out, perm.reshape(1, GROUP), blocks)
    return pl.pallas_call(
        hand_on, out_shape=shapes, in_specs=[vm] * 3, out_specs=(vm,) * 3, name="results"
    )(*results)


def solution(mesh):
    placed = (P(("seq", "blk"), None), P(), P(), P("seq"), P("seq", None), P(("seq", "blk"), None))
    return jax.shard_map(
        on_device,
        mesh=mesh,
        in_specs=placed,
        out_specs=(P(("seq", "blk"), None), P(("seq", "blk"), None), P(("seq", "blk"), None)),
        check_vma=False,
    )
```

```python
import jax
import jax.numpy as jnp
from jax import lax
from jax.experimental import pallas as pl
from jax.experimental.pallas import tpu as pltpu
from jax.sharding import PartitionSpec as P

HDIM = 64
QB = 128
GROUP = 512
SIDE = 4
BF = jnp.bfloat16
F32 = jnp.float32
MESH = pl.DeviceIdType.MESH
VMEM_BYTES = 56 * 1024 * 1024


def place():
    s = lax.axis_index("seq")
    z = lax.axis_index("blk")
    return s // 8, (s // 2) % 4, s % 2, z


def seq_of(x, y, c):
    return x * 8 + y * 2 + c


def turn(i, d):
    return lax.rem(i + (d + SIDE), SIDE)


def greet(x, y, c, z, y_steps):
    barrier = pltpu.get_barrier_semaphore()
    others = [(seq_of(x, y, c), turn(z, d)) for d in (1, 2, 3)]
    others += [(seq_of(turn(x, d), y, c), z) for d in (1, 2, 3)]
    others += [(seq_of(x, turn(y, d), c), z) for d in y_steps]
    others += [(seq_of(x, y, 1 - c), z)]
    for other in others:
        pl.semaphore_signal(barrier, inc=1, device_id=other, device_id_type=MESH)
    return lambda: pl.semaphore_wait(barrier, len(others))


def remote(src, dst, send_sem, recv_sem, device):
    return pltpu.make_async_remote_copy(
        src_ref=src,
        dst_ref=dst,
        send_sem=send_sem,
        recv_sem=recv_sem,
        device_id=device,
        device_id_type=MESH,
    )


def interleave(a, b):
    low = lax.broadcasted_iota(jnp.int32, a.shape, 1) < HDIM
    return (
        jnp.where(low, a, pltpu.roll(b, HDIM, 1)),
        jnp.where(low, pltpu.roll(a, HDIM, 1), b),
    )


def dot(a, b, ca=1, cb=0):
    return lax.dot_general(a, b, (((ca,), (cb,)), ((), ())), preferred_element_type=F32)


def store_pairs(ref, a, b):
    for half in range(2):
        cols = slice(128 * half, 128 * half + 128)
        first, second = interleave(a[:, cols], b[:, cols])
        ref[:, 256 * half : 256 * half + 128] = first.astype(BF)
        ref[:, 256 * half + 128 : 256 * half + 256] = second.astype(BF)


def plan_sums(blk_all, plan):
    shape = (QB, QB)
    lane = lax.broadcasted_iota(jnp.int32, (1, QB), 1)
    flat = jnp.zeros((1, QB), jnp.int32)
    for j in range(16):
        row = jnp.where(lane < 8, blk_all[j // 4, j % 4 : j % 4 + 1, :], 0)
        flat += pltpu.roll(row, 8 * j, 1) if j else row
    down = lax.broadcasted_iota(jnp.int32, shape, 0)
    across = lax.broadcasted_iota(jnp.int32, shape, 1)
    by_lane = jnp.broadcast_to(flat, shape)
    by_row = by_lane.T

    def total(values):
        return jnp.sum(values, axis=0, keepdims=True)

    def count(hits):
        return total(jnp.where(hits, 1, 0))

    rank = count((by_row < by_lane) | ((by_row == by_lane) & (down < across)))
    hits = jnp.broadcast_to(rank, shape).T == across
    order = total(jnp.where(hits, down, 0))
    sorted_ids = total(jnp.where(hits, by_row, 0))
    goes_on = jnp.where((sorted_ids == pltpu.roll(sorted_ids, 1, 1)) & (lane > 0), 1, 0)
    last = jnp.where(count(by_row == across) > 0, count(by_row <= across) - 1, QB)
    plan[...] = jnp.concatenate([order, goes_on, last, jnp.zeros((5, QB), jnp.int32)], axis=0)


def sublayer_kernel(
    nodes_in, w_qkv, w_out, go_in, perm, blk, out, grad_nodes, w_grad,
    nodes, go, wbuf, wobuf, pick, place_hits,
    zs_kv, zr_kv, zs_qg, zr_qg, xs_kv, xs_qg, kv_all, qg_all, blk_all, go_all,
    blk_pad, plan, plan_s, listed, keys, parts, seg, dqa,
    dkv, side, opp, y_recv, y_send, bxs_kv, bxr_kv, bxr_qa, bzs_kv, bzr_kv, bzs_qa, bzr_qa,
    mixed, gproj, gacc, wpart, wc_send, wc_recv, wx_send, wx_recv, wy_send, wy_recv, wz_send, wz_recv,
    w_sem, send, zk_r, zr_sem, xr_sem, yr_sem, rr_sem, cr_sem,
    bzr_sem, bxr_sem, byr_sem, bcr_sem, wr_sem,
):
    x, y, c, z = place()
    group = seq_of(x, y, c)
    sibling = (seq_of(x, y, 1 - c), z)
    order = (2, 1, 3, 0)
    kv_cols = pl.ds(1024, 2048)
    loads = [
        pltpu.make_async_copy(src, dst, w_sem.at[i])
        for i, (src, dst) in enumerate((
            (nodes_in, nodes),
            (w_qkv.at[:, kv_cols], wbuf.at[:, kv_cols]),
            (w_qkv.at[:, pl.ds(0, 1024)], wbuf.at[:, pl.ds(0, 1024)]),
            (go_in, go),
            (w_out, wobuf),
        ))
    ]
    for load in loads:
        load.start()
    ready = greet(x, y, c, z, (1, 2, 3))
    own_rows = pl.ds(pl.multiple_of(z * QB, QB), QB)

    def arrived(ref, sem):
        remote(ref, ref, send.at[0], sem, sibling).wait_recv()

    def sent(blocks, i):
        ref = kv_all.at[pl.ds(0, blocks)]
        remote(ref, ref, send.at[i], cr_sem.at[0], sibling).wait_send()

    def zk_copy(d, i):
        to, head = turn(z, d), turn(x, i)
        return remote(
            zs_kv.at[to, head], zr_kv.at[head, own_rows], send.at[0], zk_r.at[i], (group, to)
        )

    def z_copy(which, d):
        to = turn(z, d)
        src = zs_qg.at[to] if which == 0 else go
        dst = (zr_qg, go_all)[which].at[own_rows]
        return remote(src, dst, send.at[0], zr_sem.at[which], (group, to))

    def project(first, second, put):
        for half in range(2):
            cols = slice(128 * half, 128 * half + 128)
            a, b = interleave(first[:, cols], second[:, cols])
            put(2 * half, a.astype(BF))
            put(2 * half + 1, b.astype(BF))

    def group_rows(g):
        return kv_all.at[pl.ds(pl.multiple_of(4 * g, 4), 4)]

    def x_copy(which, d):
        to = turn(x, d)
        src = (xs_kv, xs_qg)[which].at[to]
        dst = group_rows(group) if which == 0 else qg_all.at[x]
        sem = xr_sem.at[d - 1] if which == 0 else xr_sem.at[3]
        return remote(src, dst, send.at[1 - which], sem, (seq_of(to, y, c), z))

    def y_copy(d, k, h):
        half = k if h == 0 else 1 - k
        first = pl.multiple_of(4 * seq_of(turn(x, -d), y, c) + 2 * half, 2)
        mine = kv_all.at[pl.ds(first, 2)]
        to = seq_of(x, turn(y, (1, 3)[k]), c)
        return remote(mine, mine, send.at[1], yr_sem.at[d, k, h], (to, z))

    def relay(d, k):
        step = (1, 3)[k]
        first = pl.multiple_of(4 * seq_of(turn(x, -d), turn(y, -step), c) + 2 * k, 2)
        got = kv_all.at[pl.ds(first, 2)]
        return remote(got, got, send.at[1], rr_sem.at[d], (seq_of(x, turn(y, step), c), z))

    def cross(d, k):
        got = group_rows(seq_of(turn(x, -d), turn(y, -k), c))
        return remote(got, got, send.at[1], cr_sem.at[0], sibling)

    def pass_on(d):
        for h in range(2):
            for k in range(2):
                y_copy(d, k, h).start()
        cross(d, 0).start()

    def relay_on(d):
        for k in range(2):
            y_copy(d, k, 0).wait_recv()
            relay(d, k).start()
        for k in range(2):
            y_copy(d, k, 1).wait_recv()
            cross(d, (1, 3)[k]).start()

    loads[0].wait()
    loads[1].wait()
    for d in (2, 1, 3, 0):
        to = turn(z, d)
        off = pl.multiple_of(to * 256, 256)
        k = dot(nodes[...], wbuf[:, pl.ds(1024 + off, 256)])
        v = dot(nodes[...], wbuf[:, pl.ds(2048 + off, 256)])
        if d == 2:
            ready()
        if d:
            def put(h, val):
                zs_kv[to, h] = val
            project(k, v, put)
            zk_copy(d, 0).start()
        else:
            def put(h, val):
                zr_kv[h, own_rows] = val
            project(k, v, put)
    for i in (1, 3, 2):
        for d in (2, 1, 3):
            zk_copy(d, i).start()

    local = perm[...] - group * GROUP
    hits = lax.broadcasted_iota(jnp.int32, (GROUP, GROUP), 0) == local
    one_hot = jnp.where(hits, 1.0, 0.0)
    pick[...] = one_hot.T.astype(BF)
    place_hits[...] = one_hot.astype(BF)

    blk_pad[...] = jnp.zeros_like(blk_pad)
    blk_pad[0:4, 0:8] = blk[...]
    blk_copies = [
        remote(blk_pad, blk_all.at[x], send.at[2], xr_sem.at[4], (seq_of(turn(x, d), y, c), z))
        for d in (1, 2, 3)
    ]
    for copy in blk_copies:
        copy.start()
    blk_all[x] = blk_pad[...]

    for load in loads[2:]:
        load.wait()
    for d in (2, 1, 3, 0):
        to = turn(z, d)
        off = pl.multiple_of(to * 256, 256)
        q = dot(nodes[...], wbuf[:, pl.ds(off, 256)])
        g = dot(go[...], wobuf[pl.ds(off, 256), :], 1, 1)
        if d:
            store_pairs(zs_qg.at[to], q, g)
        else:
            store_pairs(zr_qg.at[own_rows], q, g)
    go_all[own_rows] = go[...]

    for i in (0, 1, 3, 2):
        arrived(zr_kv.at[0, pl.ds(0, 3 * QB)], zk_r.at[i])
        ordered = dot(pick[...], zr_kv[turn(x, i)]).astype(BF)
        if i:
            xs_kv[turn(x, i)] = ordered.reshape(4, QB, 128)
            x_copy(0, i).start()
        else:
            kv_all[pl.ds(pl.multiple_of(4 * group, 4), 4)] = ordered.reshape(4, QB, 128)
            pass_on(0)
            for d in (2, 1, 3):
                z_copy(0, d).start()

    relay_on(0)
    for d in (1, 3, 2):
        x_copy(0, d).wait_recv()
        pass_on(d)
    relay_on(1)
    arrived(zr_qg.at[pl.ds(0, 3 * QB)], zr_sem.at[0])
    ordered = dot(pick[...], zr_qg[...])
    for h in range(SIDE):
        xs_qg[h] = ordered[:, 128 * h : 128 * h + 128].astype(BF)
    for d in (2, 1, 3):
        x_copy(1, d).start()
    for d in (2, 1, 3):
        z_copy(1, d).start()
    qg_all[x] = xs_qg[x]
    relay_on(3)

    arrived(blk_all.at[pl.ds(0, 3)], xr_sem.at[4])
    plan_sums(blk_all, plan)
    plan_copy = pltpu.make_async_copy(plan, plan_s, w_sem.at[5])
    listed_copy = pltpu.make_async_copy(blk_all, listed, w_sem.at[6])
    plan_copy.start()
    listed_copy.start()

    relay_on(2)
    for d in (0, 1, 3, 2):
        arrived(group_rows(seq_of(turn(x, -d), turn(y, 2), c)), rr_sem.at[d])
        cross(d, 2).start()
    arrived(qg_all.at[pl.ds(0, 3)], xr_sem.at[3])
    plan_copy.wait()
    listed_copy.wait()
    arrived(kv_all.at[pl.ds(0, 64)], cr_sem.at[0])

    low = lax.broadcasted_iota(jnp.int32, (QB, QB), 1) < HDIM
    top = lax.broadcasted_iota(jnp.int32, (QB, QB), 0) < HDIM
    scale = HDIM ** (-0.5)

    def softmax_and_grad(i, u, kept):
        for t in range(8):
            kept[t * QB : (t + 1) * QB] = kv_all[listed[i, u, t]]
        qg = qg_all[i, u * QB : (u + 1) * QB].astype(F32)
        both = jnp.concatenate([jnp.where(low, qg * scale, 0.0), jnp.where(low, 0.0, qg)], axis=0).astype(BF)
        rows = dot(kept[...], both, 1, 1)
        scores, grad_scores = rows[:, :QB], rows[:, QB:]
        raised = jnp.exp(scores - jnp.max(scores, axis=0, keepdims=True))
        probs = raised * (1.0 / jnp.sum(raised, axis=0, keepdims=True))
        delta = jnp.sum(probs * grad_scores, axis=0, keepdims=True)
        grad_logits = (probs * (grad_scores - delta)).astype(BF)
        return both, jnp.concatenate([grad_logits, probs.astype(BF)], axis=1)

    def bx_qa(d):
        to = turn(x, d)
        return remote(
            dqa.at[to], bxr_qa.at[x], send.at[4], bxr_sem.at[3], (seq_of(to, y, c), z)
        )

    def step(i, carry):
        pairs = [softmax_and_grad(2 * i + u // 4, u % 4, keys.at[u]) for u in range(8)]
        for u, (both, pair) in enumerate(pairs):
            back = dot(keys[u], pair, 0, 0)
            rows = slice(u % 4 * QB, u % 4 * QB + QB)
            dqa[2 * i + u // 4, rows] = jnp.where(top, back[:, :QB] * scale, back[:, QB:]).T.astype(BF)
            made = dot(pair, both).astype(BF)
            parts[pl.ds(pl.multiple_of(64 * i + 8 * u, 8), 8)] = made.reshape(8, QB, 128)
        return carry

    lax.fori_loop(0, 2, step, 0)
    for d in (2, 1, 3):
        bx_qa(d).start()
    bxr_qa[x] = dqa[x]

    def add_entry(i, run):
        run = run * plan_s[1, i].astype(F32) + parts[jnp.clip(plan_s[0, i], 0, QB - 1)].astype(F32)
        seg[i] = run
        return run

    seg[QB] = jnp.zeros((QB, 128), F32)
    lax.fori_loop(0, QB, add_entry, jnp.zeros((QB, 128), F32), unroll=4)

    def partial_sum(g, n):
        b = 4 * g + n
        return seg[jnp.clip(plan_s[2, b], 0, QB)]

    def bcross(d, k):
        return remote(dkv.at[k, d], side.at[k, d], send.at[3], bcr_sem.at[k], sibling)

    def bx_kv(d):
        to = turn(x, d)
        return remote(
            bxs_kv.at[to], bxr_kv.at[x], send.at[3], bxr_sem.at[d - 1], (seq_of(to, y, c), z)
        )

    def bzk_copy(d, i):
        to, head = turn(z, d), turn(x, i)
        rows = pl.ds(pl.multiple_of(to * QB, QB), QB)
        return remote(bzs_kv.at[head, rows], bzr_kv.at[z, head], send.at[4], bzr_sem.at[0], (group, to))

    def bzq_copy(d):
        to = turn(z, d)
        rows = pl.ds(pl.multiple_of(to * QB, QB), QB)
        return remote(bzs_qa.at[rows], bzr_qa.at[z], send.at[4], bzr_sem.at[1], (group, to))

    def opposite(d, k):
        half = pl.ds(2 * k, 2)
        return remote(
            opp.at[d, half], opp.at[SIDE + d, half], send.at[3], byr_sem.at[d],
            (seq_of(x, turn(y, (1, 3)[k]), c), z),
        )

    def beside(d, k):
        return remote(
            y_send.at[d, k], y_recv.at[d, k], send.at[3], byr_sem.at[SIDE + d],
            (seq_of(x, turn(y, (1, 3)[k]), c), z),
        )

    def paired(d, k, n):
        return partial_sum(seq_of(turn(x, d), turn(y, k), c), n) + side[k, d, n].astype(F32)

    def to_opposite(d):
        for n in range(4):
            opp[d, n] = paired(d, 2, n).astype(BF)
        opposite(d, 0).start()
        opposite(d, 1).start()

    def to_neighbours(d):
        arrived(opp.at[SIDE + d], byr_sem.at[d])
        for k in range(2):
            for n in range(4):
                total = paired(d, (1, 3)[k], n)
                if n // 2 == k:
                    total += opp[SIDE + d, n].astype(F32)
                y_send[d, k, n] = total.astype(BF)
            beside(d, k).start()

    def settle(d):
        arrived(y_recv.at[d], byr_sem.at[SIDE + d])
        for n in range(4):
            total = paired(d, 0, n) + (y_recv[d, 0, n].astype(F32) + y_recv[d, 1, n].astype(F32))
            rows = slice(QB * n, QB * n + QB)
            if d:
                bxs_kv[turn(x, d), rows] = total.astype(BF)
            else:
                bxr_kv[x, rows] = total.astype(BF)
        if d:
            bx_kv(d).start()

    def settle_z(i):
        head = turn(x, i)
        if i:
            bx_kv(SIDE - i).wait_recv()
        bzs_kv[head] = dot(place_hits[...], bxr_kv[head]).astype(BF)
        for d in (2, 1, 3):
            bzk_copy(d, i).start()
        bzr_kv[z, head] = bzs_kv[head, own_rows]

    def w_x(d):
        return remote(
            wx_send.at[turn(x, d)], wx_recv.at[d - 1],
            send.at[4], wr_sem.at[1], (seq_of(turn(x, d), y, c), z),
        )

    def w_y(d):
        return remote(
            wy_send.at[turn(y, d)], wy_recv.at[d - 1],
            send.at[4], wr_sem.at[2], (seq_of(x, turn(y, d), c), z),
        )

    def w_z(d):
        return remote(
            wz_send.at[turn(z, d)], wz_recv.at[z], send.at[5], wr_sem.at[3], (group, turn(z, d))
        )

    for k in (2, 1, 3, 0):
        for d in order:
            for n in range(4):
                dkv[k, d, n] = partial_sum(seq_of(turn(x, d), turn(y, k), 1 - c), n).astype(BF)
            bcross(d, k).start()
    arrived(side.at[2], bcr_sem.at[2])
    for d in order:
        to_opposite(d)
    arrived(side.at[1], bcr_sem.at[1])
    arrived(side.at[3], bcr_sem.at[3])
    for d in order:
        to_neighbours(d)

    arrived(bxr_qa.at[pl.ds(0, 3)], bxr_sem.at[3])
    for h in range(SIDE):
        bzs_qa[:, 128 * h : 128 * h + 128] = dot(place_hits[...], bxr_qa[h]).astype(BF)
    for d in (2, 1, 3):
        bzq_copy(d).start()
    bzr_qa[z] = bzs_qa[own_rows]

    arrived(go_all.at[pl.ds(0, 3 * QB)], zr_sem.at[1])
    group_mixed = []
    for half in range(2):
        a = bzs_qa[:, 256 * half : 256 * half + 128].astype(F32)
        b = bzs_qa[:, 256 * half + 128 : 256 * half + 256].astype(F32)
        group_mixed.append(interleave(a, b)[1].astype(BF))
    group_mixed = jnp.concatenate(group_mixed, axis=1)
    for i in range(SIDE):
        part = dot(go_all[:, 256 * i : 256 * i + 256], group_mixed, 0, 0)
        wpart[4 * i : 4 * i + 4] = part.reshape(4, 2, 32, 256)
    w_cross = remote(wc_send, wc_recv, send.at[4], wr_sem.at[0], sibling)
    wc_send[...] = wpart[:, 1 - c].astype(BF)
    w_cross.start()

    sent(60, 0)
    sent(124, 1)
    blocks_sent = blk_all.at[pl.ds(0, 3)]
    remote(blocks_sent, blocks_sent, send.at[2], xr_sem.at[4], sibling).wait_send()
    arrived(side.at[0], bcr_sem.at[0])

    settle(2)
    settle(1)
    w_cross.wait_recv()
    wsum = (wpart[:, c] + wc_recv[...].astype(F32)).reshape(SIDE, QB, 256)
    wx_send[...] = wsum.astype(BF)
    for d in (2, 1, 3):
        w_x(d).start()
    settle(3)
    settle_z(2)
    settle(0)
    settle_z(0)
    settle_z(3)
    settle_z(1)

    wrows = wx_send[x].astype(F32)
    arrived(wx_recv, wr_sem.at[1])
    for d in (1, 2, 3):
        wrows += wx_recv[d - 1].astype(F32)
    wy_send[...] = wrows.reshape(SIDE, 32, 256)
    for d in (2, 1, 3):
        w_y(d).start()

    arrived(bzr_qa.at[pl.ds(0, 3)], bzr_sem.at[1])
    for h in range(SIDE):
        for half in range(2):
            a = bzr_qa[h, :, 256 * half : 256 * half + 128].astype(F32)
            b = bzr_qa[h, :, 256 * half + 128 : 256 * half + 256].astype(F32)
            cols = slice(256 * h + 128 * half, 256 * h + 128 * half + 128)
            first, second = interleave(a, b)
            gproj[:, cols] = first.astype(BF)
            mixed[:, cols] = second.astype(BF)
    out[...] = dot(mixed[...], wobuf[...]).astype(BF)
    for i in range(SIDE):
        rows = slice(256 * i, 256 * i + 256)
        gacc[:, rows] = dot(gproj[:, :1024], wbuf[rows, :1024], 1, 1)

    wrows = wy_send[y]
    arrived(wy_recv, wr_sem.at[2])
    for d in (1, 2, 3):
        wrows += wy_recv[d - 1]
    wz_send[...] = wrows.reshape(SIDE, 8, 256)
    for d in (2, 1, 3):
        w_z(d).start()
    wz_recv[z] = wz_send[z]

    arrived(bzr_kv.at[pl.ds(0, 3)], bzr_sem.at[0])
    for h in range(SIDE):
        for half in range(2):
            a = bzr_kv[h, 2 * half].astype(F32)
            b = bzr_kv[h, 2 * half + 1].astype(F32)
            col = 256 * h + 128 * half
            first, second = interleave(a, b)
            gproj[:, 1024 + col : 1024 + col + 128] = first.astype(BF)
            gproj[:, 2048 + col : 2048 + col + 128] = second.astype(BF)
    for i in range(SIDE):
        rows = slice(256 * i, 256 * i + 256)
        grad_nodes[:, rows] = (gacc[:, rows] + dot(gproj[:, 1024:], wbuf[rows, 1024:], 1, 1)).astype(BF)

    arrived(wz_recv.at[pl.ds(0, 3)], wr_sem.at[3])
    for h in range(SIDE):
        w_grad[:, 256 * h : 256 * h + 256] = wz_recv[h]

    sent(124, 3)
    sent(53, 4)
    third = wz_send.at[pl.ds(0, 3)]
    remote(third, third, send.at[5], wr_sem.at[3], sibling).wait_send()


def hand_on(*refs):
    half = len(refs) // 2
    for i in range(half):
        refs[half + i][...] = refs[i][...]


def dma(*shape):
    return pltpu.SemaphoreType.DMA(shape)


def low_precision(*shape):
    return pltpu.VMEM(shape, BF)


def full(*shape):
    return pltpu.VMEM(shape, F32)


def on_device(nodes, w_qkv, w_out, perm, blocks, grad_out):
    vm = pl.BlockSpec(memory_space=pltpu.VMEM)
    anywhere = pl.BlockSpec(memory_space=pl.ANY)
    sds = jax.ShapeDtypeStruct
    shapes = (sds((QB, 1024), BF), sds((QB, 1024), BF), sds((8, 1024), F32))
    low = low_precision
    heads = (SIDE, GROUP, 128)
    results = pl.pallas_call(
        sublayer_kernel,
        out_shape=shapes,
        in_specs=[anywhere, anywhere, anywhere, anywhere, vm, vm],
        out_specs=(vm, vm, vm),
        scratch_shapes=[
            low(QB, 1024), low(QB, 1024), low(1024, 3072), low(1024, 1024), low(GROUP, GROUP), low(GROUP, GROUP),
            low(SIDE, SIDE, QB, 128), low(*heads), low(SIDE, QB, 512), low(GROUP, 512),
            low(SIDE, 4, QB, 128), low(*heads), low(QB, QB, 128), low(*heads),
            pltpu.VMEM((SIDE, 8, 128), jnp.int32), low(GROUP, 1024),
            pltpu.VMEM((8, QB), jnp.int32), pltpu.VMEM((8, QB), jnp.int32), pltpu.SMEM((8, QB), jnp.int32), pltpu.SMEM((SIDE, 8, 128), jnp.int32),
            low(8, 1024, 128), low(QB, QB, 128), full(QB + 1, QB, 128), low(*heads),
            low(SIDE, SIDE, 4, QB, 128), low(SIDE, SIDE, 4, QB, 128), low(2 * SIDE, 4, QB, 128),
            low(SIDE, 2, 4, QB, 128), low(SIDE, 2, 4, QB, 128),
            low(*heads), low(*heads), low(*heads), low(*heads), low(SIDE, SIDE, QB, 128),
            low(GROUP, 512), low(SIDE, QB, 512),
            low(QB, 1024), low(QB, 3072), full(QB, 1024), full(16, 2, 32, 256), low(16, 32, 256), low(16, 32, 256),
            low(SIDE, QB, 256), low(3, QB, 256), full(SIDE, 32, 256), full(3, 32, 256),
            full(SIDE, 8, 256), full(SIDE, 8, 256),
            dma(7), dma(6), dma(4), dma(2), dma(5), dma(4, 2, 2), dma(4), dma(1),
            dma(2), dma(4), dma(8), dma(4), dma(4),
        ],
        compiler_params=pltpu.CompilerParams(
            collective_id=0, has_side_effects=True, vmem_limit_bytes=VMEM_BYTES
        ),
        name="sublayer",
    )(nodes, w_qkv, w_out, grad_out, perm.reshape(1, GROUP), blocks)
    return pl.pallas_call(
        hand_on, out_shape=shapes, in_specs=[vm] * 3, out_specs=(vm,) * 3, name="results"
    )(*results)


def solution(mesh):
    placed = (P(("seq", "blk"), None), P(), P(), P("seq"), P("seq", None), P(("seq", "blk"), None))
    return jax.shard_map(
        on_device,
        mesh=mesh,
        in_specs=placed,
        out_specs=(P(("seq", "blk"), None), P(("seq", "blk"), None), P(("seq", "blk"), None)),
        check_vma=False,
    )
```

```python
import jax
import jax.numpy as jnp
from jax import lax
from jax.experimental import pallas as pl
from jax.experimental.pallas import tpu as pltpu
from jax.sharding import PartitionSpec as P

HDIM = 64
QB = 128
GROUP = 512
SIDE = 4
BF = jnp.bfloat16
F32 = jnp.float32
MESH = pl.DeviceIdType.MESH
VMEM_BYTES = 56 * 1024 * 1024


def place():
    s = lax.axis_index("seq")
    z = lax.axis_index("blk")
    return s // 8, (s // 2) % 4, s % 2, z


def seq_of(x, y, c):
    return x * 8 + y * 2 + c


def turn(i, d):
    return lax.rem(i + (d + SIDE), SIDE)


def greet(x, y, c, z, y_steps):
    barrier = pltpu.get_barrier_semaphore()
    others = [(seq_of(x, y, c), turn(z, d)) for d in (1, 2, 3)]
    others += [(seq_of(turn(x, d), y, c), z) for d in (1, 2, 3)]
    others += [(seq_of(x, turn(y, d), c), z) for d in y_steps]
    others += [(seq_of(x, y, 1 - c), z)]
    for other in others:
        pl.semaphore_signal(barrier, inc=1, device_id=other, device_id_type=MESH)
    return lambda: pl.semaphore_wait(barrier, len(others))


def remote(src, dst, send_sem, recv_sem, device):
    return pltpu.make_async_remote_copy(
        src_ref=src,
        dst_ref=dst,
        send_sem=send_sem,
        recv_sem=recv_sem,
        device_id=device,
        device_id_type=MESH,
    )


def interleave(a, b):
    low = lax.broadcasted_iota(jnp.int32, a.shape, 1) < HDIM
    return (
        jnp.where(low, a, pltpu.roll(b, HDIM, 1)),
        jnp.where(low, pltpu.roll(a, HDIM, 1), b),
    )


def dot(a, b, ca=1, cb=0):
    return lax.dot_general(a, b, (((ca,), (cb,)), ((), ())), preferred_element_type=F32)


def store_pairs(ref, a, b):
    for half in range(2):
        cols = slice(128 * half, 128 * half + 128)
        first, second = interleave(a[:, cols], b[:, cols])
        ref[:, 256 * half : 256 * half + 128] = first.astype(BF)
        ref[:, 256 * half + 128 : 256 * half + 256] = second.astype(BF)


def plan_sums(blk_all, plan):
    shape = (QB, QB)
    lane = lax.broadcasted_iota(jnp.int32, (1, QB), 1)
    flat = jnp.zeros((1, QB), jnp.int32)
    for j in range(16):
        row = jnp.where(lane < 8, blk_all[j // 4, j % 4 : j % 4 + 1, :], 0)
        flat += pltpu.roll(row, 8 * j, 1) if j else row
    down = lax.broadcasted_iota(jnp.int32, shape, 0)
    across = lax.broadcasted_iota(jnp.int32, shape, 1)
    by_lane = jnp.broadcast_to(flat, shape)
    by_row = by_lane.T

    def total(values):
        return jnp.sum(values, axis=0, keepdims=True)

    def count(hits):
        return total(jnp.where(hits, 1, 0))

    rank = count((by_row < by_lane) | ((by_row == by_lane) & (down < across)))
    hits = jnp.broadcast_to(rank, shape).T == across
    order = total(jnp.where(hits, down, 0))
    sorted_ids = total(jnp.where(hits, by_row, 0))
    goes_on = jnp.where((sorted_ids == pltpu.roll(sorted_ids, 1, 1)) & (lane > 0), 1, 0)
    last = jnp.where(count(by_row == across) > 0, count(by_row <= across) - 1, QB)
    plan[...] = jnp.concatenate([order, goes_on, last, jnp.zeros((5, QB), jnp.int32)], axis=0)


def sublayer_kernel(
    nodes_in, w_qkv, w_out, go_in, perm, blk, out, grad_nodes, w_grad,
    nodes, go, wbuf, wobuf, pick, place_hits,
    zs_kv, zr_kv, zs_qg, zr_qg, xs_kv, xs_qg, kv_all, qg_all, blk_all, go_all,
    blk_pad, plan, plan_s, listed, keys, parts, seg, dqa,
    dkv, side, opp, y_recv, y_send, bxs_kv, bxr_kv, bxr_qa, bzs_kv, bzr_kv, bzs_qa, bzr_qa,
    mixed, gproj, gacc, wpart, wc_send, wc_recv, wx_send, wx_recv, wy_send, wy_recv, wz_send, wz_recv,
    w_sem, send, zk_r, zr_sem, xr_sem, yr_sem, rr_sem, cr_sem,
    bzr_sem, bxr_sem, byr_sem, bcr_sem, wr_sem,
):
    x, y, c, z = place()
    group = seq_of(x, y, c)
    sibling = (seq_of(x, y, 1 - c), z)
    order = (2, 1, 3, 0)

    def load(i, src, dst):
        copy = pltpu.make_async_copy(src, dst, w_sem.at[i])
        copy.start()
        return copy

    def load_cols(i, first, width):
        cols = pl.ds(pl.multiple_of(first, 256), width)
        return load(i, w_qkv.at[:, cols], wbuf.at[:, cols])

    load_nodes = load(0, nodes_in, nodes)
    load_kv = [
        [load_cols(7 + 2 * i + j, 1024 * j + 1024 + 256 * turn(z, d), 256) for j in range(2)]
        for i, d in enumerate(order)
    ]
    loads = [load(1, go_in, go), load_cols(2, 0, 1024), load(3, w_out, wobuf)]
    ready = greet(x, y, c, z, (1, 2, 3))
    own_rows = pl.ds(pl.multiple_of(z * QB, QB), QB)

    def arrived(ref, sem):
        remote(ref, ref, send.at[0], sem, sibling).wait_recv()

    def sent(blocks, i):
        ref = kv_all.at[pl.ds(0, blocks)]
        remote(ref, ref, send.at[i], cr_sem.at[0], sibling).wait_send()

    def zk_copy(d, i):
        to, head = turn(z, d), turn(x, i)
        return remote(
            zs_kv.at[to, head], zr_kv.at[head, own_rows], send.at[0], zk_r.at[i], (group, to)
        )

    def z_copy(which, d):
        to = turn(z, d)
        src = zs_qg.at[to] if which == 0 else go
        dst = (zr_qg, go_all)[which].at[own_rows]
        return remote(src, dst, send.at[0], zr_sem.at[which], (group, to))

    def project(first, second, put):
        for half in range(2):
            cols = slice(128 * half, 128 * half + 128)
            a, b = interleave(first[:, cols], second[:, cols])
            put(2 * half, a.astype(BF))
            put(2 * half + 1, b.astype(BF))

    def group_rows(g):
        return kv_all.at[pl.ds(pl.multiple_of(4 * g, 4), 4)]

    def x_copy(which, d):
        to = turn(x, d)
        src = (xs_kv, xs_qg)[which].at[to]
        dst = group_rows(group) if which == 0 else qg_all.at[x]
        sem = xr_sem.at[d - 1] if which == 0 else xr_sem.at[3]
        return remote(src, dst, send.at[1 - which], sem, (seq_of(to, y, c), z))

    def y_copy(d, k, h):
        half = k if h == 0 else 1 - k
        first = pl.multiple_of(4 * seq_of(turn(x, -d), y, c) + 2 * half, 2)
        mine = kv_all.at[pl.ds(first, 2)]
        to = seq_of(x, turn(y, (1, 3)[k]), c)
        return remote(mine, mine, send.at[1], yr_sem.at[d, k, h], (to, z))

    def relay(d, k):
        step = (1, 3)[k]
        first = pl.multiple_of(4 * seq_of(turn(x, -d), turn(y, -step), c) + 2 * k, 2)
        got = kv_all.at[pl.ds(first, 2)]
        return remote(got, got, send.at[1], rr_sem.at[d], (seq_of(x, turn(y, step), c), z))

    def cross(d, k):
        got = group_rows(seq_of(turn(x, -d), turn(y, -k), c))
        return remote(got, got, send.at[1], cr_sem.at[0], sibling)

    def pass_on(d):
        for h in range(2):
            for k in range(2):
                y_copy(d, k, h).start()
        cross(d, 0).start()

    def relay_on(d):
        for k in range(2):
            y_copy(d, k, 0).wait_recv()
            relay(d, k).start()
        for k in range(2):
            y_copy(d, k, 1).wait_recv()
            cross(d, (1, 3)[k]).start()

    load_nodes.wait()
    for i, d in enumerate(order):
        to = turn(z, d)
        off = pl.multiple_of(to * 256, 256)
        for copy in load_kv[i]:
            copy.wait()
        k = dot(nodes[...], wbuf[:, pl.ds(1024 + off, 256)])
        v = dot(nodes[...], wbuf[:, pl.ds(2048 + off, 256)])
        if d == 2:
            ready()
        if d:
            def put(h, val):
                zs_kv[to, h] = val
            project(k, v, put)
            zk_copy(d, 0).start()
        else:
            def put(h, val):
                zr_kv[h, own_rows] = val
            project(k, v, put)
    for i in (1, 3, 2):
        for d in (2, 1, 3):
            zk_copy(d, i).start()

    local = perm[...] - group * GROUP
    hits = lax.broadcasted_iota(jnp.int32, (GROUP, GROUP), 0) == local
    one_hot = jnp.where(hits, 1.0, 0.0)
    pick[...] = one_hot.T.astype(BF)
    place_hits[...] = one_hot.astype(BF)

    blk_pad[...] = jnp.zeros_like(blk_pad)
    blk_pad[0:4, 0:8] = blk[...]
    blk_copies = [
        remote(blk_pad, blk_all.at[x], send.at[2], xr_sem.at[4], (seq_of(turn(x, d), y, c), z))
        for d in (1, 2, 3)
    ]
    for copy in blk_copies:
        copy.start()
    blk_all[x] = blk_pad[...]

    for copy in loads:
        copy.wait()
    for d in (2, 1, 3, 0):
        to = turn(z, d)
        off = pl.multiple_of(to * 256, 256)
        q = dot(nodes[...], wbuf[:, pl.ds(off, 256)])
        g = dot(go[...], wobuf[pl.ds(off, 256), :], 1, 1)
        if d:
            store_pairs(zs_qg.at[to], q, g)
        else:
            store_pairs(zr_qg.at[own_rows], q, g)
    go_all[own_rows] = go[...]

    for i in (0, 1, 3, 2):
        arrived(zr_kv.at[0, pl.ds(0, 3 * QB)], zk_r.at[i])
        ordered = dot(pick[...], zr_kv[turn(x, i)]).astype(BF)
        if i:
            xs_kv[turn(x, i)] = ordered.reshape(4, QB, 128)
            x_copy(0, i).start()
        else:
            kv_all[pl.ds(pl.multiple_of(4 * group, 4), 4)] = ordered.reshape(4, QB, 128)
            pass_on(0)
            for d in (2, 1, 3):
                z_copy(0, d).start()

    relay_on(0)
    for d in (1, 3, 2):
        x_copy(0, d).wait_recv()
        pass_on(d)
    relay_on(1)
    arrived(zr_qg.at[pl.ds(0, 3 * QB)], zr_sem.at[0])
    ordered = dot(pick[...], zr_qg[...])
    for h in range(SIDE):
        xs_qg[h] = ordered[:, 128 * h : 128 * h + 128].astype(BF)
    for d in (2, 1, 3):
        x_copy(1, d).start()
    for d in (2, 1, 3):
        z_copy(1, d).start()
    qg_all[x] = xs_qg[x]
    relay_on(3)

    arrived(blk_all.at[pl.ds(0, 3)], xr_sem.at[4])
    plan_sums(blk_all, plan)
    plan_copy = pltpu.make_async_copy(plan, plan_s, w_sem.at[5])
    listed_copy = pltpu.make_async_copy(blk_all, listed, w_sem.at[6])
    plan_copy.start()
    listed_copy.start()

    relay_on(2)
    for d in (0, 1, 3, 2):
        arrived(group_rows(seq_of(turn(x, -d), turn(y, 2), c)), rr_sem.at[d])
        cross(d, 2).start()
    arrived(qg_all.at[pl.ds(0, 3)], xr_sem.at[3])
    plan_copy.wait()
    listed_copy.wait()
    arrived(kv_all.at[pl.ds(0, 64)], cr_sem.at[0])

    low = lax.broadcasted_iota(jnp.int32, (QB, QB), 1) < HDIM
    top = lax.broadcasted_iota(jnp.int32, (QB, QB), 0) < HDIM
    scale = HDIM ** (-0.5)

    def softmax_and_grad(i, u, kept):
        for t in range(8):
            kept[t * QB : (t + 1) * QB] = kv_all[listed[i, u, t]]
        qg = qg_all[i, u * QB : (u + 1) * QB].astype(F32)
        both = jnp.concatenate([jnp.where(low, qg * scale, 0.0), jnp.where(low, 0.0, qg)], axis=0).astype(BF)
        rows = dot(kept[...], both, 1, 1)
        scores, grad_scores = rows[:, :QB], rows[:, QB:]
        raised = jnp.exp(scores - jnp.max(scores, axis=0, keepdims=True))
        probs = raised * (1.0 / jnp.sum(raised, axis=0, keepdims=True))
        delta = jnp.sum(probs * grad_scores, axis=0, keepdims=True)
        grad_logits = (probs * (grad_scores - delta)).astype(BF)
        return both, jnp.concatenate([grad_logits, probs.astype(BF)], axis=1)

    def bx_qa(d):
        to = turn(x, d)
        return remote(
            dqa.at[to], bxr_qa.at[x], send.at[4], bxr_sem.at[3], (seq_of(to, y, c), z)
        )

    def step(i, carry):
        pairs = [softmax_and_grad(2 * i + u // 4, u % 4, keys.at[u]) for u in range(8)]
        for u, (both, pair) in enumerate(pairs):
            back = dot(keys[u], pair, 0, 0)
            rows = slice(u % 4 * QB, u % 4 * QB + QB)
            dqa[2 * i + u // 4, rows] = jnp.where(top, back[:, :QB] * scale, back[:, QB:]).T.astype(BF)
            made = dot(pair, both).astype(BF)
            parts[pl.ds(pl.multiple_of(64 * i + 8 * u, 8), 8)] = made.reshape(8, QB, 128)
        return carry

    lax.fori_loop(0, 2, step, 0)
    for d in (2, 1, 3):
        bx_qa(d).start()
    bxr_qa[x] = dqa[x]

    def add_entry(i, run):
        run = run * plan_s[1, i].astype(F32) + parts[jnp.clip(plan_s[0, i], 0, QB - 1)].astype(F32)
        seg[i] = run
        return run

    seg[QB] = jnp.zeros((QB, 128), F32)
    lax.fori_loop(0, QB, add_entry, jnp.zeros((QB, 128), F32), unroll=4)

    def partial_sum(g, n):
        b = 4 * g + n
        return seg[jnp.clip(plan_s[2, b], 0, QB)]

    def bcross(d, k):
        return remote(dkv.at[k, d], side.at[k, d], send.at[3], bcr_sem.at[SIDE + d if k == 2 else k], sibling)

    def bx_kv(d):
        to = turn(x, d)
        return remote(
            bxs_kv.at[to], bxr_kv.at[x], send.at[3], bxr_sem.at[d - 1], (seq_of(to, y, c), z)
        )

    def bzk_copy(d, i):
        to, head = turn(z, d), turn(x, i)
        rows = pl.ds(pl.multiple_of(to * QB, QB), QB)
        return remote(bzs_kv.at[head, rows], bzr_kv.at[z, head], send.at[4], bzr_sem.at[0], (group, to))

    def bzq_copy(d):
        to = turn(z, d)
        rows = pl.ds(pl.multiple_of(to * QB, QB), QB)
        return remote(bzs_qa.at[rows], bzr_qa.at[z], send.at[4], bzr_sem.at[1], (group, to))

    def opposite(d, k):
        half = pl.ds(2 * k, 2)
        return remote(
            opp.at[d, half], opp.at[SIDE + d, half], send.at[3], byr_sem.at[d],
            (seq_of(x, turn(y, (1, 3)[k]), c), z),
        )

    def beside(d, k):
        return remote(
            y_send.at[d, k], y_recv.at[d, k], send.at[3], byr_sem.at[SIDE + d],
            (seq_of(x, turn(y, (1, 3)[k]), c), z),
        )

    def paired(d, k, n):
        return partial_sum(seq_of(turn(x, d), turn(y, k), c), n) + side[k, d, n].astype(F32)

    def to_opposite(d):
        for n in range(4):
            opp[d, n] = paired(d, 2, n).astype(BF)
        opposite(d, 0).start()
        opposite(d, 1).start()

    def to_neighbours(d):
        arrived(opp.at[SIDE + d], byr_sem.at[d])
        for k in range(2):
            for n in range(4):
                total = paired(d, (1, 3)[k], n)
                if n // 2 == k:
                    total += opp[SIDE + d, n].astype(F32)
                y_send[d, k, n] = total.astype(BF)
            beside(d, k).start()

    def settle(d):
        arrived(y_recv.at[d], byr_sem.at[SIDE + d])
        for n in range(4):
            total = paired(d, 0, n) + (y_recv[d, 0, n].astype(F32) + y_recv[d, 1, n].astype(F32))
            rows = slice(QB * n, QB * n + QB)
            if d:
                bxs_kv[turn(x, d), rows] = total.astype(BF)
            else:
                bxr_kv[x, rows] = total.astype(BF)
        if d:
            bx_kv(d).start()

    def settle_z(i):
        head = turn(x, i)
        if i:
            bx_kv(SIDE - i).wait_recv()
        bzs_kv[head] = dot(place_hits[...], bxr_kv[head]).astype(BF)
        for d in (2, 1, 3):
            bzk_copy(d, i).start()
        bzr_kv[z, head] = bzs_kv[head, own_rows]

    def w_x(d):
        return remote(
            wx_send.at[turn(x, d)], wx_recv.at[d - 1],
            send.at[4], wr_sem.at[1], (seq_of(turn(x, d), y, c), z),
        )

    def w_y(d):
        return remote(
            wy_send.at[turn(y, d)], wy_recv.at[d - 1],
            send.at[4], wr_sem.at[2], (seq_of(x, turn(y, d), c), z),
        )

    def w_z(d):
        return remote(
            wz_send.at[turn(z, d)], wz_recv.at[z], send.at[5], wr_sem.at[3], (group, turn(z, d))
        )

    for k in (2, 1, 3, 0):
        for d in order:
            for n in range(4):
                dkv[k, d, n] = partial_sum(seq_of(turn(x, d), turn(y, k), 1 - c), n).astype(BF)
            bcross(d, k).start()
    for d in order:
        arrived(side.at[2, d], bcr_sem.at[SIDE + d])
        to_opposite(d)
    arrived(side.at[1], bcr_sem.at[1])
    arrived(side.at[3], bcr_sem.at[3])
    for d in order:
        to_neighbours(d)

    arrived(bxr_qa.at[pl.ds(0, 3)], bxr_sem.at[3])
    for h in range(SIDE):
        bzs_qa[:, 128 * h : 128 * h + 128] = dot(place_hits[...], bxr_qa[h]).astype(BF)
    for d in (2, 1, 3):
        bzq_copy(d).start()
    bzr_qa[z] = bzs_qa[own_rows]

    arrived(go_all.at[pl.ds(0, 3 * QB)], zr_sem.at[1])
    group_mixed = []
    for half in range(2):
        a = bzs_qa[:, 256 * half : 256 * half + 128].astype(F32)
        b = bzs_qa[:, 256 * half + 128 : 256 * half + 256].astype(F32)
        group_mixed.append(interleave(a, b)[1].astype(BF))
    group_mixed = jnp.concatenate(group_mixed, axis=1)
    for i in range(SIDE):
        part = dot(go_all[:, 256 * i : 256 * i + 256], group_mixed, 0, 0)
        wpart[4 * i : 4 * i + 4] = part.reshape(4, 2, 32, 256)
    w_cross = remote(wc_send, wc_recv, send.at[4], wr_sem.at[0], sibling)
    wc_send[...] = wpart[:, 1 - c].astype(BF)
    w_cross.start()

    sent(60, 0)
    sent(124, 1)
    blocks_sent = blk_all.at[pl.ds(0, 3)]
    remote(blocks_sent, blocks_sent, send.at[2], xr_sem.at[4], sibling).wait_send()
    arrived(side.at[0], bcr_sem.at[0])

    settle(2)
    settle(1)
    w_cross.wait_recv()
    wsum = (wpart[:, c] + wc_recv[...].astype(F32)).reshape(SIDE, QB, 256)
    wx_send[...] = wsum.astype(BF)
    for d in (2, 1, 3):
        w_x(d).start()
    settle(3)
    settle_z(2)
    settle(0)
    settle_z(0)
    settle_z(3)
    settle_z(1)

    wrows = wx_send[x].astype(F32)
    arrived(wx_recv, wr_sem.at[1])
    for d in (1, 2, 3):
        wrows += wx_recv[d - 1].astype(F32)
    wy_send[...] = wrows.reshape(SIDE, 32, 256)
    for d in (2, 1, 3):
        w_y(d).start()

    arrived(bzr_qa.at[pl.ds(0, 3)], bzr_sem.at[1])
    for h in range(SIDE):
        for half in range(2):
            a = bzr_qa[h, :, 256 * half : 256 * half + 128].astype(F32)
            b = bzr_qa[h, :, 256 * half + 128 : 256 * half + 256].astype(F32)
            cols = slice(256 * h + 128 * half, 256 * h + 128 * half + 128)
            first, second = interleave(a, b)
            gproj[:, cols] = first.astype(BF)
            mixed[:, cols] = second.astype(BF)
    out[...] = dot(mixed[...], wobuf[...]).astype(BF)
    for i in range(SIDE):
        rows = slice(256 * i, 256 * i + 256)
        gacc[:, rows] = dot(gproj[:, :1024], wbuf[rows, :1024], 1, 1)

    wrows = wy_send[y]
    arrived(wy_recv, wr_sem.at[2])
    for d in (1, 2, 3):
        wrows += wy_recv[d - 1]
    wz_send[...] = wrows.reshape(SIDE, 8, 256)
    for d in (2, 1, 3):
        w_z(d).start()
    wz_recv[z] = wz_send[z]

    arrived(bzr_kv.at[pl.ds(0, 3)], bzr_sem.at[0])
    for h in range(SIDE):
        for half in range(2):
            a = bzr_kv[h, 2 * half].astype(F32)
            b = bzr_kv[h, 2 * half + 1].astype(F32)
            col = 256 * h + 128 * half
            first, second = interleave(a, b)
            gproj[:, 1024 + col : 1024 + col + 128] = first.astype(BF)
            gproj[:, 2048 + col : 2048 + col + 128] = second.astype(BF)
    for i in range(SIDE):
        rows = slice(256 * i, 256 * i + 256)
        grad_nodes[:, rows] = (gacc[:, rows] + dot(gproj[:, 1024:], wbuf[rows, 1024:], 1, 1)).astype(BF)

    arrived(wz_recv.at[pl.ds(0, 3)], wr_sem.at[3])
    for h in range(SIDE):
        w_grad[:, 256 * h : 256 * h + 256] = wz_recv[h]

    sent(124, 3)
    sent(53, 4)
    third = wz_send.at[pl.ds(0, 3)]
    remote(third, third, send.at[5], wr_sem.at[3], sibling).wait_send()


def hand_on(*refs):
    half = len(refs) // 2
    for i in range(half):
        refs[half + i][...] = refs[i][...]


def dma(*shape):
    return pltpu.SemaphoreType.DMA(shape)


def low_precision(*shape):
    return pltpu.VMEM(shape, BF)


def full(*shape):
    return pltpu.VMEM(shape, F32)


def on_device(nodes, w_qkv, w_out, perm, blocks, grad_out):
    vm = pl.BlockSpec(memory_space=pltpu.VMEM)
    anywhere = pl.BlockSpec(memory_space=pl.ANY)
    sds = jax.ShapeDtypeStruct
    shapes = (sds((QB, 1024), BF), sds((QB, 1024), BF), sds((8, 1024), F32))
    low = low_precision
    heads = (SIDE, GROUP, 128)
    results = pl.pallas_call(
        sublayer_kernel,
        out_shape=shapes,
        in_specs=[anywhere, anywhere, anywhere, anywhere, vm, vm],
        out_specs=(vm, vm, vm),
        scratch_shapes=[
            low(QB, 1024), low(QB, 1024), low(1024, 3072), low(1024, 1024), low(GROUP, GROUP), low(GROUP, GROUP),
            low(SIDE, SIDE, QB, 128), low(*heads), low(SIDE, QB, 512), low(GROUP, 512),
            low(SIDE, 4, QB, 128), low(*heads), low(QB, QB, 128), low(*heads),
            pltpu.VMEM((SIDE, 8, 128), jnp.int32), low(GROUP, 1024),
            pltpu.VMEM((8, QB), jnp.int32), pltpu.VMEM((8, QB), jnp.int32), pltpu.SMEM((8, QB), jnp.int32), pltpu.SMEM((SIDE, 8, 128), jnp.int32),
            low(8, 1024, 128), low(QB, QB, 128), full(QB + 1, QB, 128), low(*heads),
            low(SIDE, SIDE, 4, QB, 128), low(SIDE, SIDE, 4, QB, 128), low(2 * SIDE, 4, QB, 128),
            low(SIDE, 2, 4, QB, 128), low(SIDE, 2, 4, QB, 128),
            low(*heads), low(*heads), low(*heads), low(*heads), low(SIDE, SIDE, QB, 128),
            low(GROUP, 512), low(SIDE, QB, 512),
            low(QB, 1024), low(QB, 3072), full(QB, 1024), full(16, 2, 32, 256), low(16, 32, 256), low(16, 32, 256),
            low(SIDE, QB, 256), low(3, QB, 256), full(SIDE, 32, 256), full(3, 32, 256),
            full(SIDE, 8, 256), full(SIDE, 8, 256),
            dma(15), dma(6), dma(4), dma(2), dma(5), dma(4, 2, 2), dma(4), dma(1),
            dma(2), dma(4), dma(8), dma(8), dma(4),
        ],
        compiler_params=pltpu.CompilerParams(
            collective_id=0, has_side_effects=True, vmem_limit_bytes=VMEM_BYTES
        ),
        name="sublayer",
    )(nodes, w_qkv, w_out, grad_out, perm.reshape(1, GROUP), blocks)
    return pl.pallas_call(
        hand_on, out_shape=shapes, in_specs=[vm] * 3, out_specs=(vm,) * 3, name="results"
    )(*results)


def solution(mesh):
    placed = (P(("seq", "blk"), None), P(), P(), P("seq"), P("seq", None), P(("seq", "blk"), None))
    return jax.shard_map(
        on_device,
        mesh=mesh,
        in_specs=placed,
        out_specs=(P(("seq", "blk"), None), P(("seq", "blk"), None), P(("seq", "blk"), None)),
        check_vma=False,
    )
```
